128 devices in a mesh: dp: 4 (over z), expert: 32 (over x, y, core).
Axes of the slice: x: 4, y: 4, z: 4, core: 2. Of those that a mesh axis runs over, the one named last changes fastest.
Arguments:
- attn_prefill: bfloat16 [15360, 2048], P(('dp', 'expert')), may hold values from -6 to 6
- decode_held: bfloat16 [512, 2048], P(('dp', 'expert')), may hold values from -6 to 6
- decode_source: int32 [512], P(('dp', 'expert')), may hold values from 0 to 15, as said below
- residual: bfloat16 [15872, 2048], P(('dp', 'expert')), may hold values from -6 to 6
- live_rows: int32 [128], P(('dp', 'expert')), may hold values from 1 to 120, 11520 in all
- expert_ids: int32 [15872, 6], P(('dp', 'expert')), may hold values from 0 to 31, all different within a row; in each aligned block of 124 rows (0 to 123, 124 to 247, ...) at most 24 rows name the same one
- replica_pick: int32 [128, 32], P(('dp', 'expert')), may hold values from 0 to 3
- w_out: bfloat16 [2048, 2048], P(None, 'dp'), may hold values from -0.125 to 0.125
- norm_gain: float32 [2048], replicated, may hold values from 0.5 to 1.5
- router: bfloat16 [2048, 32], replicated, may hold values from -8 to 8
- exp_gate: bfloat16 [32, 2048, 1408], P('expert'), may hold values from -0.125 to 0.125
- exp_up: bfloat16 [32, 2048, 1408], P('expert'), may hold values from -0.125 to 0.125
- exp_down: bfloat16 [32, 1408, 2048], P('expert'), may hold values from -0.15625 to 0.15625
- shared_gate: bfloat16 [1408, 2048], P('dp'), may hold values from -0.125 to 0.125
- shared_up: bfloat16 [1408, 2048], P('dp'), may hold values from -0.125 to 0.125
- shared_down: bfloat16 [1408, 2048], P('dp'), may hold values from -0.15625 to 0.15625
Outputs:
- out: bfloat16 [15872, 2048], P(('dp', 'expert'))
- copy_rows: int32 [128], P(('dp', 'expert'))
The draws below stay inside these ranges and needn't reach their ends.
Inputs may be any that keep to these rules, and one draw needn't show every extreme that they name: `expert_ids`: each row names 6 different experts; within the rows of one device no expert is named by more than 24 rows, and in some or all devices one expert is named by exactly 24 rows. `live_rows`: the values sum to 11520, and the largest is exactly 120. `decode_source`: for each index c of expert, the entries of the devices (r, c), taken in order of r, are a permutation of 0 .. 15.
All inputs are finite; a program needn't handle non-finite values.
Results may differ from the reference program's by a relative error of at most 0.01.
Values may be sent and summed in bfloat16 or wider, within the bound.
A program may use at most 128 MiB of HBM per device.

```python
import math
import jax
import jax.numpy as jnp
import numpy as np
from jax import lax

D = 2048
FFE = 1408
SHF = 1408
EXPERTS = 32
TOP = 6
PRE_DEV = 120
DEC_DEV = 4
ROWS_DEV = 124
MOST = 24
TOK_PRE = 15360
TOK_DEC = 512
TOKENS = 15872
N_DP = 4
N_EXPERT = 32
DEVICES = 128


def draw_decode_source(key, part):
    keys = jax.random.split(jax.random.fold_in(key, 5), N_EXPERT)
    orders = jax.vmap(lambda one_key: jax.random.permutation(one_key, N_DP * DEC_DEV))(keys)
    return orders.reshape(N_EXPERT, N_DP, DEC_DEV).transpose(1, 0, 2).reshape(N_DP * N_EXPERT * DEC_DEV).astype(jnp.int32)


def draw_router(key, part):
    key = jax.random.fold_in(key, 11)
    values = jax.random.truncated_normal(jax.random.fold_in(key, 1), -4.0, 4.0, (D, EXPERTS), jnp.float32) * (0.5 / math.sqrt(D))
    return jnp.clip(values, -8.0, 8.0).astype(jnp.bfloat16)


def set_ends(drawn, key, smallest, largest):
    longest = drawn.shape.index(max(drawn.shape))
    spots = []
    for shift in (0, 1):
        where = [jax.random.randint(jax.random.fold_in(key, axis), (), 0, length) for axis, length in enumerate(drawn.shape)]
        where[longest] = (where[longest] + shift) % drawn.shape[longest]
        spots.append(tuple(where))
    return drawn.at[spots[0]].set(smallest).at[spots[1]].set(largest)


def levels(key, dims, pieces, smallest, largest):
    gain = 1.0
    for dim, blocks in pieces:
        draws = jax.random.uniform(jax.random.fold_in(jax.random.fold_in(key, 6), dim), (blocks,), jnp.float32, smallest / len(pieces), largest / len(pieces))
        gain = gain * jnp.repeat(jnp.exp(draws), dims[dim] // blocks).reshape((-1,) + (1,) * (len(dims) - 1 - dim))
    return gain


def split_up(amount, total, bound, slope):
    weights = [(1 << 20) // math.isqrt(grade ** slope) + 1 for grade in range(2, amount + 1)]
    spare, given = total - bound - (amount - 1), [1] * (amount - 1)
    while spare > 0:
        candidates = [i for i in range(amount - 1) if given[i] < bound]
        mass, budget = sum([weights[i] for i in candidates]), spare
        for i in candidates:
            addition = min(bound - given[i], max(1, budget * weights[i] // mass), spare)
            given[i] = given[i] + addition
            spare = spare - addition
    return np.array([bound] + given)


def uneven_parts(stream_key, number_of, total, reach, skew):
    if number_of == 2:
        one = jax.random.randint(stream_key, (), max(1, total - reach), min(reach, total - 1) + 1)
        return jnp.stack([one, total - one])
    lengths = jnp.asarray(split_up(number_of, total, reach, skew), jnp.int32)
    couples = (number_of - 1) // 2
    source_of, receiver = lengths[1:1 + 2 * couples:2], lengths[2:2 + 2 * couples:2]
    margin = jnp.minimum(source_of - 1, reach - receiver)
    moved = jax.random.randint(jax.random.fold_in(stream_key, 1), (couples,), 0, 1 << 20) % (margin + 1)
    lengths = lengths.at[1:1 + 2 * couples:2].set(source_of - moved).at[2:2 + 2 * couples:2].set(receiver + moved)
    return lengths[jax.random.permutation(jax.random.fold_in(stream_key, 2), number_of)]


def routed_block(own_key, own, number, rows, amount, top, reach, skew):
    sequence = jax.random.permutation(own_key, amount)
    heavy_load, ordinary = portions_of(amount, rows * top, reach, skew, True), portions_of(amount, rows * top, reach, skew, False)
    places = jnp.arange(amount)

    def named(lengths, rotation):
        used = int((lengths > 0).sum())
        fixed = max(1, used // 4)
        shifted = fixed + (places - fixed + rotation * (used - fixed)) % max(1, amount - fixed)
        return jnp.zeros((amount,), jnp.int32).at[sequence[jnp.where(places < fixed, places, shifted)]].set(jnp.asarray(lengths, jnp.int32))

    lengths = jnp.where(number % 4 == 0, named(heavy_load, number // 4), named(ordinary, number - number // 4 - 1))
    mixed = jax.random.permutation(jax.random.fold_in(own, 3), amount)
    source_of, taker = mixed[0:amount // 2 * 2:2], mixed[1:amount // 2 * 2:2]
    slack = jnp.minimum(lengths[source_of] - 1, reach - lengths[taker]) // 2
    slack = jnp.where((source_of == sequence[0]) | (taker == sequence[0]) | (lengths[taker] == 0), 0, jnp.maximum(slack, 0))
    shifted = jax.random.randint(jax.random.fold_in(own, 4), (amount // 2,), 0, 1 << 20) % (slack + 1)
    lengths = lengths.at[source_of].add(-shifted).at[taker].add(shifted)
    labels = jnp.searchsorted(jnp.cumsum(lengths), jnp.arange(rows * top), side="right").astype(jnp.int32)
    listing = labels.reshape(top, rows).T
    listing = listing[jax.random.permutation(jax.random.fold_in(own, 1), rows)]
    rotation = jax.random.randint(jax.random.fold_in(own, 2), (rows, 1), 0, top)
    return jnp.take_along_axis(listing, (jnp.arange(top)[None, :] + rotation) % top, axis=1)


def portions_of(count, total, reach, lean, full):
    weights = [(1 << 20) // math.isqrt(grade ** lean) + 1 for grade in range(1, count + 1)]
    largest = reach if full else min(reach, max(-(-total // count), total * weights[0] // sum(weights)))
    least = 1 if total - largest >= count - 1 else 0
    holding, surplus = [largest] + [least] * (count - 1), total - largest - least * (count - 1)
    while surplus > 0:
        movable = [i for i in range(1, count) if holding[i] < largest] or [i for i in range(1, count) if holding[i] < reach]
        whole, remaining = sum([weights[i] for i in movable]), surplus
        for i in movable:
            more = min(reach - holding[i], max(1, remaining * weights[i] // whole), surplus)
            holding[i] = holding[i] + more
            surplus = surplus - more
    return np.array(holding)


def normal_values(rng, shape, spread, bound, cuts=(), held_as=jnp.bfloat16):
    entries = spread * jax.random.normal(rng, shape, jnp.float32)
    if cuts:
        entries = entries * levels(rng, shape, cuts, -0.22, 0.18)
    return jnp.clip(entries, -bound, bound).astype(held_as)


def setup_inputs(seed: int = 0) -> dict:
    key_list = jax.random.split(jax.random.key(seed), 17)
    attn_prefill = normal_values(key_list[0], (TOK_PRE, D), 1.0, 6.0, ((0, 128),))
    decode_held = normal_values(key_list[1], (TOK_DEC, D), 1.0, 6.0, ((0, 128),))
    decode_source = draw_decode_source(jax.random.fold_in(key_list[16], 71), 0)
    residual = normal_values(key_list[3], (TOKENS, D), 1.0, 6.0, ((0, 128),))
    live_rows = uneven_parts(key_list[4], DEVICES, DEVICES * PRE_DEV * 3 // 4, PRE_DEV, 2).astype(jnp.int32)
    expert_ids_keys = jax.random.split(jax.random.fold_in(key_list[5], 1), TOKENS // ROWS_DEV)
    expert_ids_turns = jax.random.permutation(jax.random.fold_in(key_list[5], 3), TOKENS // ROWS_DEV)
    expert_ids = jax.vmap(lambda own, number: routed_block(jax.random.fold_in(key_list[5], 2), own, number, ROWS_DEV, EXPERTS, TOP, MOST, 2))(expert_ids_keys, expert_ids_turns).reshape((TOKENS, TOP))
    replica_pick = set_ends(jax.random.randint(key_list[6], (DEVICES, EXPERTS), 0, N_DP), jax.random.fold_in(key_list[6], 1), 0, N_DP - 1).astype(jnp.int32)
    w_out = normal_values(key_list[7], (D, D), D ** -0.5, 0.125, ((1, 4),))
    norm_gain = jnp.clip(1.0 + 0.1 * jax.random.normal(key_list[8], (D,), jnp.float32), 0.5, 1.5)
    router = draw_router(jax.random.fold_in(key_list[16], 71), 0)
    exp_gate = normal_values(key_list[10], (EXPERTS, D, FFE), D ** -0.5, 0.125, ((0, 32),))
    exp_up = normal_values(key_list[11], (EXPERTS, D, FFE), D ** -0.5, 0.125, ((0, 32),))
    exp_down = normal_values(key_list[12], (EXPERTS, FFE, D), FFE ** -0.5, 0.15625, ((0, 32),))
    shared_gate = normal_values(key_list[13], (SHF, D), D ** -0.5, 0.125, ((0, 4),))
    shared_up = normal_values(key_list[14], (SHF, D), D ** -0.5, 0.125, ((0, 4),))
    shared_down = normal_values(key_list[15], (SHF, D), SHF ** -0.5, 0.15625, ((0, 4),))
    return {"attn_prefill": attn_prefill, "decode_held": decode_held, "decode_source": decode_source, "residual": residual, "live_rows": live_rows, "expert_ids": expert_ids, "replica_pick": replica_pick, "w_out": w_out, "norm_gain": norm_gain, "router": router, "exp_gate": exp_gate, "exp_up": exp_up, "exp_down": exp_down, "shared_gate": shared_gate, "shared_up": shared_up, "shared_down": shared_down}


EPSILON = 1e-06

def reference(attn_prefill, decode_held, decode_source, residual, live_rows, expert_ids, replica_pick, w_out, norm_gain, router, exp_gate, exp_up, exp_down, shared_gate, shared_up, shared_down):
    held = decode_held.reshape(N_DP, N_EXPERT, DEC_DEV, D).transpose(1, 0, 2, 3).reshape(N_EXPERT, N_DP * DEC_DEV, D)
    source = decode_source.reshape(N_DP, N_EXPERT, DEC_DEV).transpose(1, 0, 2).reshape(N_EXPERT, N_DP * DEC_DEV)
    picked = jax.vmap(lambda rows_held, rows_source: jnp.take(rows_held, rows_source, axis=0))(held, source)
    decode_rows = picked.reshape(N_EXPERT, N_DP, DEC_DEV, D).transpose(1, 0, 2, 3).reshape(DEVICES, DEC_DEV, D)
    attn_all = jnp.concatenate([attn_prefill.reshape(DEVICES, PRE_DEV, D), decode_rows], axis=1).reshape(TOKENS, D)
    projected = jnp.dot(attn_all, w_out, preferred_element_type=jnp.float32).astype(jnp.bfloat16)
    hidden = residual.astype(jnp.float32) + projected.astype(jnp.float32)
    inverse_rms = lax.rsqrt(lax.optimization_barrier(jnp.mean(hidden * hidden, axis=1, keepdims=True)) + EPSILON)
    normed = (hidden * inverse_rms * norm_gain[None, :]).astype(jnp.bfloat16)
    expert_probs = jax.nn.softmax(jnp.dot(normed, router, preferred_element_type=jnp.float32), axis=1)
    device_of = jnp.arange(TOKENS) // ROWS_DEV
    slot_of = jnp.arange(TOKENS) % ROWS_DEV
    row_live = (slot_of < live_rows[device_of]) | (slot_of >= PRE_DEV)
    contract = (((1,), (1,)), ((), ()))
    shared_gate_part = lax.dot_general(normed, shared_gate, contract, preferred_element_type=jnp.float32)
    shared_up_part = lax.dot_general(normed, shared_up, contract, preferred_element_type=jnp.float32)
    shared_inner = (jax.nn.silu(shared_gate_part) * shared_up_part).astype(jnp.bfloat16)
    shared_out = jnp.dot(shared_inner, shared_down, preferred_element_type=jnp.float32)
    position = jnp.arange(DEVICES * MOST)

    def add_expert(expert_index, running):
        chosen = jnp.any(expert_ids == expert_index, axis=1) & row_live
        picked_rows = jnp.nonzero(chosen, size=DEVICES * MOST, fill_value=0)[0]
        valid = (position < jnp.sum(chosen.astype(jnp.int32))).astype(jnp.float32)
        weight = expert_probs[picked_rows, expert_index] * valid
        rows_in = normed[picked_rows]
        gate_part = jnp.dot(rows_in, exp_gate[expert_index], preferred_element_type=jnp.float32)
        up_part = jnp.dot(rows_in, exp_up[expert_index], preferred_element_type=jnp.float32)
        expert_inner = (jax.nn.silu(gate_part) * up_part).astype(jnp.bfloat16)
        expert_out = jnp.dot(expert_inner, exp_down[expert_index], preferred_element_type=jnp.float32).astype(jnp.bfloat16)
        expert_out = lax.optimization_barrier(expert_out).astype(jnp.float32)
        return running.at[picked_rows].add(weight[:, None] * expert_out)
    routed = lax.fori_loop(0, EXPERTS, add_expert, jnp.zeros((TOKENS, D), jnp.float32))
    out = (hidden + shared_out + routed).astype(jnp.bfloat16)
    choice_hits = ((expert_ids[:, :, None] == jnp.arange(EXPERTS)[None, None, :]) & row_live[:, None, None]).astype(jnp.int32)
    per_source = lax.optimization_barrier(jnp.sum(choice_hits.reshape(DEVICES, ROWS_DEV * TOP, EXPERTS), axis=1))
    dp_rows = jnp.arange(N_DP, dtype=jnp.int32)[:, None, None]
    offset = (dp_rows - replica_pick[None, :, :].astype(jnp.int32)) % N_DP
    served_each = (per_source[None] - offset + N_DP - 1) // N_DP
    served = lax.optimization_barrier(jnp.sum(served_each, axis=1))
    copy_rows = lax.optimization_barrier(jnp.sum(served.reshape(N_DP, N_EXPERT, EXPERTS // N_EXPERT), axis=2)).reshape(DEVICES).astype(jnp.int32)
    return (out, copy_rows)
```

```python
import functools

import jax
import jax.numpy as jnp
from jax import lax
from jax.experimental import pallas as pl
from jax.experimental.pallas import tpu as pltpu
from jax.sharding import PartitionSpec as P

EPSILON = 1e-06
MESH = pl.DeviceIdType.MESH
BF = jnp.bfloat16
F32 = jnp.float32
NT = (((1,), (1,)), ((), ()))
TN = (((0,), (0,)), ((), ()))

Z_AG, Z_RET, Z_HELD, CODE_A, CODE_B, CR_Z, CR_X, CR_Y, CR_K = 0, 6, 9, 12, 15, 18, 21, 24, 27
PROB_A, PROB_B, X_AG, Y_AG, S_AG, DIS_A, DIS_B, S_RS = 28, 31, 34, 40, 46, 52, 60, 68
RET_A, RET_B, SUM_A, SUM_B, COPIES = 71, 79, 87, 90, 93


def dot(a, b):
    return jnp.dot(a, b, preferred_element_type=F32)


def iota(shape, dim):
    return lax.broadcasted_iota(jnp.int32, shape, dim)


def kernel(
    pre, held, source, resid, live, ids, pick, w_out_h, gain, router_t, wg_h, wu_h, wd_h, sg_h, su_h, sd_h,
    out, copy_rows,
    w_out, wg, wu, wd, sg, su, sd,
    hid, zb, pb, pr, hps, hr, idsp, code_a, code_b, ca, cb, svt, crz, crx, cry, crk, crs,
    prob_a, prob_b, pa, pb_b, buf_a, buf_b, sb, sp, sr, onehot, s2a, s2b, r2a, r2b, inner_a, inner_b,
    r3a, r3b, wca, wcb, s4a, s4b, r4a, r4b,
    ss, rs, ws, ls,
):
    a = lax.axis_index("dp")
    c = lax.axis_index("expert")
    x, y, k = c // 8, lax.rem(c // 2, 4), lax.rem(c, 2)

    def at(z_, x_, y_, k_):
        return (z_, (x_ * 4 + y_) * 2 + k_)

    def m4(v):
        return lax.rem(v, 4)

    loads = [
        pltpu.make_async_copy(src, dst, ws.at[i])
        for i, (src, dst) in enumerate(
            [(w_out_h, w_out), (sg_h, sg), (su_h, su), (sd_h, sd), (wg_h.at[0], wg), (wu_h.at[0], wu), (wd_h.at[0], wd)]
        )
    ]
    for load in loads:
        load.start()

    sent, finished = [], set()

    def send(i, src, dst, device):
        copy = pltpu.make_async_remote_copy(
            src_ref=src, dst_ref=dst, send_sem=ss.at[i], recv_sem=rs.at[i], device_id=device, device_id_type=MESH
        )
        copy.start()
        sent.append(copy)
        return copy

    zdev = lambda i: at(i, x, y, k)
    xdev = lambda i: at(a, i, y, k)
    ydev = lambda i: at(a, x, i, k)

    def others(me, base, dev, src, dst):
        return [send(base + i - 1, src(m4(me + i)), dst(m4(me + i)), dev(m4(me + i))) for i in (1, 2, 3)]

    def ring(base, buf, me, dev):
        right, left = m4(me + 1), m4(me + 3)
        top, bottom = pl.ds(0, 64), pl.ds(64, 64)
        go = lambda i, slot, part, to: send(base + i, buf.at[slot, part], buf.at[slot, part], dev(to))
        copies = [go(0, me, top, right), go(1, me, bottom, left), go(2, me, bottom, right), go(3, me, top, left)]

        def forward():
            copies[0].wait_recv()
            copies.append(go(4, left, top, right))
            copies[1].wait_recv()
            copies.append(go(5, right, bottom, left))

        return copies, forward

    hid[0:120, :] = pre[...].astype(F32)
    hid[120:128, :] = jnp.zeros((8, 2048), F32)
    hid[120:124, :] = held[...].astype(F32)
    zb[a] = hid[...].astype(BF)

    barrier = pltpu.get_barrier_semaphore()
    peers = [at(m4(a + i), x, y, k) for i in (1, 2, 3)]
    peers += [at(a, x, m4(y + i), lax.rem(k + j, 2)) for i in range(4) for j in range(2) if i or j]
    peers += [at(a, m4(x + i), y, lax.rem(k + j, 2)) for i in (1, 2, 3) for j in range(2)]
    for peer in peers:
        pl.semaphore_signal(barrier, inc=1, device_id=peer, device_id_type=MESH)
    pl.semaphore_wait(barrier, len(peers))

    z_copies, z_forward = ring(Z_AG, zb, a, zdev)

    idsp[...] = jnp.full((8, 128), -1, jnp.int32)
    idsp[0:6, 0:124] = ids[...]
    lane = iota((32, 128), 1)
    row = iota((32, 128), 0)
    alive = (lane < live[0]) | (lane >= 120)
    before = jnp.where(iota((128, 128), 0) < iota((128, 128), 1), 1.0, 0.0).astype(BF)

    def match(expert):
        hit = idsp[0:1, :] == expert
        for i in range(1, 6):
            hit = hit | (idsp[i : i + 1, :] == expert)
        return jnp.where(hit & alive, 1.0, 0.0)

    hits = match(row)
    ranks = dot(hits.astype(BF), before)
    code_a[...] = jnp.where(hits > 0.5, ranks + (24 * x).astype(F32), -1.0)
    hits_b = match(lax.rem(row // 2, 4) * 8 + row // 8 * 2 + lax.rem(row, 2))
    ranks_b = dot(hits_b.astype(BF), before)
    code_b[...] = jnp.where(hits_b > 0.5, ranks_b + (24 * y).astype(F32), -1.0)

    def tile(ref, i):
        return ref.at[pl.ds(pl.multiple_of(i * 8, 8), 8)]

    ca[x] = code_a[pl.ds(pl.multiple_of(x * 8, 8), 8), :]
    cb[y] = code_b[pl.ds(pl.multiple_of(y * 8, 8), 8), :]
    code_copies = others(x, CODE_A, xdev, lambda i: tile(code_a, i), lambda i: ca.at[x])
    code_copies += others(y, CODE_B, ydev, lambda i: tile(code_b, i), lambda i: cb.at[y])

    counts = lax.dot_general(jnp.ones((8, 128), BF), hits.astype(BF), NT, preferred_element_type=F32)
    copy_index = iota((8, 32), 0)
    offset = lax.rem(copy_index - pick[...] + 4, 4)
    served = (counts.astype(jnp.int32) - offset + 3) // 4
    svt[...] = jnp.zeros((8, 128), F32)
    svt[:, 0:32] = jnp.where(copy_index < 4, served, 0).astype(F32)
    crz[a] = svt[...]
    cr_copies = others(a, CR_Z, zdev, lambda i: svt, lambda i: crz.at[a])

    loads[0].wait()

    def project(slot):
        pb[slot] = dot(zb[slot], w_out[...]).astype(BF)

    project(a)
    pr[a] = pb[a]
    left, right, opposite = m4(a + 3), m4(a + 1), m4(a + 2)
    z_forward()
    returns = []
    for i, (slot, parts) in enumerate(((left, (2,)), (right, (3,)), (opposite, (4, 5)))):
        for part in parts:
            z_copies[part].wait_recv()
        project(slot)
        returns.append(send(Z_RET + i, pb.at[slot], pr.at[a], zdev(slot)))
    place_row, place_col = iota((16, 512), 0), iota((16, 512), 1)
    place_t = lax.rem(place_col, 128)
    place = (place_t >= 120) & (place_t < 124) & (place_row == place_col // 128 * 4 + place_t - 120)
    hps[...] = dot(jnp.where(place, 1.0, 0.0).astype(BF), pb[...].reshape(512, 512)).astype(BF)
    hr[a] = hps[...]
    returns += others(a, Z_HELD, zdev, lambda i: hps, lambda i: hr.at[a])

    for copy in cr_copies:
        copy.wait_recv()
    crs[0] = crz[0] + crz[1] + crz[2] + crz[3]
    crx[x] = crs[0]
    cr_copies = others(x, CR_X, xdev, lambda i: crs.at[0], lambda i: crx.at[x])

    hid[120:128, :] = jnp.zeros((8, 2048), F32)
    hid[0:124, :] = resid[...].astype(F32)
    sel_t, sel_i = iota((128, 16), 0), iota((128, 16), 1)
    chosen = jnp.full((128, 16), -1, jnp.int32)
    for i in range(4):
        chosen = jnp.where(sel_t == 120 + i, source[i], chosen)
    select = jnp.where(sel_i == chosen, 1.0, 0.0).astype(BF)
    prefill = iota((128, 512), 0) < 120
    for copy in returns:
        copy.wait_recv()
    for i in range(4):
        cols = slice(i * 512, i * 512 + 512)
        hid[:, cols] = hid[:, cols] + jnp.where(prefill, pr[i].astype(F32), dot(select, hr[i]))

    def norm(i, _):
        rows = pl.ds(pl.multiple_of(i * 16, 16), 16)
        v = hid[rows, :]
        scale = lax.rsqrt(jnp.mean(v * v, axis=1, keepdims=True) + EPSILON)
        normed = (v * scale * gain[...]).astype(BF)
        buf_a[x, rows, :] = normed[:, 0:1024]
        buf_b[y, rows, :] = normed[:, 1024:2048]
        sb[a, rows, :] = normed
        return 0

    lax.fori_loop(0, 8, norm, 0)
    x_copies, x_forward = ring(X_AG, buf_a, x, xdev)
    y_copies, y_forward = ring(Y_AG, buf_b, y, ydev)
    s_copies, s_forward = ring(S_AG, sb, a, zdev)

    logits = lax.dot_general(router_t[...], sb[a], NT, preferred_element_type=F32)
    powers = jnp.exp(logits - jnp.max(logits, axis=0, keepdims=True))
    prob_a[...] = powers / jnp.sum(powers, axis=0, keepdims=True)
    for i in range(16):
        j = i % 4 * 4 + i // 4
        prob_b[2 * i : 2 * i + 2, :] = prob_a[2 * j : 2 * j + 2, :]
    pa[x] = prob_a[pl.ds(pl.multiple_of(x * 8, 8), 8), :]
    pb_b[y] = prob_b[pl.ds(pl.multiple_of(y * 8, 8), 8), :]
    prob_copies = others(x, PROB_A, xdev, lambda i: tile(prob_a, i), lambda i: pa.at[x])
    prob_copies += others(y, PROB_B, ydev, lambda i: tile(prob_b, i), lambda i: pb_b.at[y])

    x_forward()
    y_forward()
    for copy in cr_copies:
        copy.wait_recv()
    crs[1] = crx[0] + crx[1] + crx[2] + crx[3]
    cry[y] = crs[1]
    cr_copies = others(y, CR_Y, ydev, lambda i: crs.at[1], lambda i: cry.at[y])
    for copy in code_copies:
        copy.wait_recv()

    slot96 = iota((96, 512), 0).astype(F32)

    def codes(ref, i):
        return jnp.concatenate([ref[s, pl.ds(i, 1), :] for s in range(4)], axis=1)

    locals_ = []

    def dispatch(base, step, core, code, buf, slots, landing, me, dev, group):
        for i in range(4):
            onehot[96 * i : 96 * i + 96, :] = jnp.where(slot96 == codes(code, 2 * i + core), 1.0, 0.0).astype(BF)

        def columns(n, _):
            cols = pl.ds(pl.multiple_of(n * 256, 256), 256)
            rows = buf[:, :, cols].reshape(512, 256)
            slots[core, :, :, cols] = dot(onehot[...], rows).astype(BF).reshape(4, 96, 256)
            return 0

        lax.fori_loop(0, 4, columns, 0)
        copies = []
        for i in range(4):
            to = m4(me + i)
            if step == 0 and i == 0:
                copy = pltpu.make_async_copy(slots.at[core, to], landing.at[k, me], ls.at[base])
                copy.start()
                locals_.append(copy)
                continue
            copies.append(send(group + 4 * step + i, slots.at[core, to], landing.at[k, me], dev(to, core)))
        return copies

    col_dev = lambda i, core: at(a, x, i, core)
    row_dev = lambda i, core: at(a, i, y, core)
    for copy in x_copies[2:]:
        copy.wait_recv()
    arrive = [[], []]
    arrive[0] += dispatch(0, 0, k, ca, buf_a, s2a, r2a, y, col_dev, DIS_A)
    for copy in y_copies[2:]:
        copy.wait_recv()
    arrive[0] += dispatch(1, 0, k, cb, buf_b, s2b, r2b, x, row_dev, DIS_B)
    arrive[1] += dispatch(0, 1, 1 - k, ca, buf_a, s2a, r2a, y, col_dev, DIS_A)
    arrive[1] += dispatch(1, 1, 1 - k, cb, buf_b, s2b, r2b, x, row_dev, DIS_B)

    s_forward()
    for copy in s_copies[2:]:
        copy.wait_recv()
    for load in loads[1:4]:
        load.wait()

    def shared(i, _):
        rows = sb[i]
        gate = lax.dot_general(rows, sg[...], NT, preferred_element_type=F32)
        up = lax.dot_general(rows, su[...], NT, preferred_element_type=F32)
        hidden_units = (gate / (1.0 + jnp.exp(-gate)) * up).astype(BF)

        def columns(n, _):
            cols = pl.ds(pl.multiple_of(n * 512, 512), 512)
            sp[i, :, cols] = dot(hidden_units, sd[:, cols]).astype(BF)
            return 0

        lax.fori_loop(0, 4, columns, 0)
        return 0

    lax.fori_loop(0, 4, shared, 0)
    shared_copies = others(a, S_RS, zdev, lambda i: sp.at[i], lambda i: sr.at[a])
    sr[a] = sp[a]

    for copy in prob_copies:
        copy.wait_recv()

    def weights(code, prob, into):
        for i in range(8):
            e = lax.rem(i, 4) * 2 + i // 4
            hit = slot96 == codes(code, e)
            into[96 * i : 96 * i + 96, :] = jnp.where(hit, codes(prob, e), 0.0).astype(BF)

    weights(ca, pa, wca)
    weights(cb, pb_b, wcb)

    for copy in cr_copies:
        copy.wait_recv()
    crs[2] = cry[0] + cry[1] + cry[2] + cry[3]
    crk[k] = crs[2]
    cr_copy = send(CR_K, crs.at[2], crk.at[k], at(a, x, y, 1 - k))

    for load in loads[4:]:
        load.wait()

    def swapped(v):
        return jnp.concatenate([v[(j * 4 + i) * 24 : (j * 4 + i) * 24 + 24] for i in range(4) for j in range(4)], axis=0)

    def expert(step, core):
        for copy in arrive[step]:
            copy.wait_recv()
        if step == 0:
            for copy in locals_:
                copy.wait()

        def up(n, _):
            cols = pl.ds(pl.multiple_of(n * 128, 128), 128)
            first = jnp.concatenate([wg[0:1024, cols], wu[0:1024, cols]], axis=1)
            second = jnp.concatenate([wg[1024:2048, cols], wu[1024:2048, cols]], axis=1)
            h = dot(r2a[core].reshape(384, 1024), first) + swapped(dot(r2b[core].reshape(384, 1024), second))
            gate = h[:, 0:128]
            inner = gate / (1.0 + jnp.exp(-gate)) * h[:, 128:256]
            inner_a[:, cols] = inner.astype(BF)
            inner_b[:, cols] = swapped(inner).astype(BF)
            return 0

        lax.fori_loop(0, 11, up, 0)
        for copy in arrive[step]:
            copy.wait_send()
            finished.add(id(copy))
        copies = []
        for group, inner, slots, landing, me, dev, first in (
            (RET_A, inner_a, s2a, r3a, y, col_dev, 0),
            (RET_B, inner_b, s2b, r3b, x, row_dev, 1024),
        ):

            def down(n, _):
                cols = pl.ds(pl.multiple_of(n * 256, 256), 256)
                wide = pl.ds(pl.multiple_of(first + n * 256, 256), 256)
                slots[core, :, :, cols] = dot(inner[...], wd[:, wide]).astype(BF).reshape(4, 96, 256)
                return 0

            lax.fori_loop(0, 4, down, 0)
            for i in range(4):
                to = m4(me + i)
                if step == 0 and i == 0:
                    copy = pltpu.make_async_copy(slots.at[core, to], landing.at[k, me], ls.at[2 + (group == RET_B)])
                    copy.start()
                    locals_.append(copy)
                    continue
                copies.append(send(group + 4 * step + i, slots.at[core, to], landing.at[k, me], dev(to, core)))
        return copies

    back = expert(0, k)
    back += expert(1, 1 - k)
    back_a, back_b = [back[i] for i in (0, 1, 2, 6, 7, 8, 9)], [back[i] for i in (3, 4, 5, 10, 11, 12, 13)]

    def combine(copies, local, wc, landed, sums, finals, me, dev, group):
        for copy in copies:
            copy.wait_recv()
        local.wait()

        def columns(n, _):
            cols = pl.ds(pl.multiple_of(n * 256, 256), 256)
            v = lax.dot_general(wc[...], landed[:, :, :, cols].reshape(768, 256), TN, preferred_element_type=F32)
            sums[:, :, cols] = v.astype(BF).reshape(4, 128, 256)
            return 0

        lax.fori_loop(0, 4, columns, 0)
        finals[me] = sums[me]
        return others(me, group, dev, lambda i: sums.at[i], lambda i: finals.at[me])

    last = combine(back_a, locals_[2], wca, r3a, s4a, r4a, x, xdev, SUM_A)
    last += combine(back_b, locals_[3], wcb, r3b, s4b, r4b, y, ydev, SUM_B)

    cr_copy.wait_recv()
    served_all = crk[0] + crk[1]
    mine = (iota((8, 128), 0) == a) & (iota((8, 128), 1) == c)
    copy_rows[0] = jnp.sum(jnp.where(mine, served_all, 0.0)).astype(jnp.int32)

    for copy in shared_copies + last:
        copy.wait_recv()
    for finals, first in ((r4a, 0), (r4b, 1024)):

        def total(n, _):
            cols = pl.ds(pl.multiple_of(n * 256, 256), 256)
            wide = pl.ds(pl.multiple_of(first + n * 256, 256), 256)
            v = hid[:, wide]
            for i in range(4):
                v = v + sr[i, :, wide].astype(F32)
            for i in range(4):
                v = v + finals[i, :, cols].astype(F32)
            out[:, wide] = v[0:124].astype(BF)
            return 0

        lax.fori_loop(0, 4, total, 0)
    for copy in sent:
        if id(copy) not in finished:
            copy.wait_send()


def body(
    attn_prefill, decode_held, decode_source, residual, live_rows, expert_ids, replica_pick, w_out, norm_gain, router,
    exp_gate, exp_up, exp_down, shared_gate, shared_up, shared_down,
):
    vmem = pl.BlockSpec(memory_space=pltpu.VMEM)
    smem = pl.BlockSpec(memory_space=pltpu.SMEM)
    hbm = pl.BlockSpec(memory_space=pl.ANY)
    V = pltpu.VMEM
    return pl.pallas_call(
        kernel,
        out_shape=(jax.ShapeDtypeStruct((124, 2048), BF), jax.ShapeDtypeStruct((1,), jnp.int32)),
        in_specs=[vmem, vmem, smem, vmem, smem, vmem, vmem, hbm, vmem, vmem, hbm, hbm, hbm, hbm, hbm, hbm],
        out_specs=(vmem, smem),
        scratch_shapes=[
            V((2048, 512), BF), V((2048, 1408), BF), V((2048, 1408), BF), V((1408, 2048), BF),
            V((352, 2048), BF), V((352, 2048), BF), V((352, 2048), BF),
            V((128, 2048), F32), V((4, 128, 2048), BF), V((4, 128, 512), BF), V((4, 128, 512), BF),
            V((16, 512), BF), V((4, 16, 512), BF),
            V((8, 128), jnp.int32), V((32, 128), F32), V((32, 128), F32), V((4, 8, 128), F32), V((4, 8, 128), F32),
            V((8, 128), F32), V((4, 8, 128), F32), V((4, 8, 128), F32), V((4, 8, 128), F32), V((2, 8, 128), F32),
            V((3, 8, 128), F32),
            V((32, 128), F32), V((32, 128), F32), V((4, 8, 128), F32), V((4, 8, 128), F32),
            V((4, 128, 1024), BF), V((4, 128, 1024), BF),
            V((4, 128, 2048), BF), V((4, 128, 2048), BF), V((4, 128, 2048), BF),
            V((384, 512), BF),
            V((2, 4, 96, 1024), BF), V((2, 4, 96, 1024), BF), V((2, 4, 96, 1024), BF), V((2, 4, 96, 1024), BF),
            V((384, 1408), BF), V((384, 1408), BF),
            V((2, 4, 96, 1024), BF), V((2, 4, 96, 1024), BF),
            V((768, 512), BF), V((768, 512), BF),
            V((4, 128, 1024), BF), V((4, 128, 1024), BF), V((4, 128, 1024), BF), V((4, 128, 1024), BF),
            pltpu.SemaphoreType.DMA((COPIES,)), pltpu.SemaphoreType.DMA((COPIES,)),
            pltpu.SemaphoreType.DMA((7,)), pltpu.SemaphoreType.DMA((4,)),
        ],
        compiler_params=pltpu.CompilerParams(collective_id=0, has_side_effects=True, vmem_limit_bytes=62 << 20),
        cost_estimate=pl.CostEstimate(flops=17_000_000_000, bytes_accessed=26_000_000, transcendentals=2_000_000),
        name="moe",
    )(
        attn_prefill, decode_held, decode_source, residual, live_rows, expert_ids.T, replica_pick, w_out,
        norm_gain.reshape(1, 2048), router.T, exp_gate, exp_up, exp_down, shared_gate, shared_up, shared_down,
    )


def solution(mesh):
    rows = P(("dp", "expert"), None)
    flat = P(("dp", "expert"))
    placed = (
        rows, rows, flat, rows, flat, rows, rows, P(None, "dp"), P(), P(),
        P("expert", None, None), P("expert", None, None), P("expert", None, None),
        P("dp", None), P("dp", None), P("dp", None),
    )
    return jax.shard_map(body, mesh=mesh, in_specs=placed, out_specs=(rows, flat), check_vma=False)
```

```python
import functools

import jax
import jax.numpy as jnp
from jax import lax
from jax.experimental import pallas as pl
from jax.experimental.pallas import tpu as pltpu
from jax.sharding import PartitionSpec as P

EPSILON = 1e-06
MESH = pl.DeviceIdType.MESH
BF = jnp.bfloat16
F32 = jnp.float32
NT = (((1,), (1,)), ((), ()))

GROUPS = dict(
    Z_TOP=2, Z_BOTTOM=2, Z_RET=2, HELD=3, W_PIECE=2, WA_X=6, WA_Y=6, WB_Y=6, WB_X=6, W_CORE=2, CODE_A=3, CODE_B=3, CR_Z=3,
    CR_X=3, CR_Y=3, CR_K=1, PROB_A=3, PROB_B=3, X_AG=6, Y_AG=6, S_AG=6, DIS_A=8, DIS_B=8, S_SUM=6, RET_A=8, RET_B=8, SUM_A=6, SUM_B=6,
)
COPIES = sum(GROUPS.values())
ID = {name: sum(list(GROUPS.values())[:i]) for i, name in enumerate(GROUPS)}


def dot(a, b):
    return jnp.dot(a, b, preferred_element_type=F32)


def iota(shape, dim):
    return lax.broadcasted_iota(jnp.int32, shape, dim)


def kernel(
    pre, held, source, resid, live, ids, pick, w_out_h, gain, router_t, wg_h, wu_h, wd_h, sg_h, su_h, sd_h,
    out, copy_rows,
    w_out, wg, wu, wd, sg, su, sd,
    hid, zb, pb, pr, held_f, held_s, held_all, wo_a, wo_b, idsp, code_a, code_b, ca, cb, svt, crz, crx, cry, crk, crs,
    prob_a, prob_b, pa, pb_b, buf_a, buf_b, sb, sp, s_mid, sr, onehot, s2a, s2b, r2a, r2b, inner_a, inner_b,
    r3a, r3b, wide, wca, wcb, s4a, s4b, mid_a, mid_b, r4a, r4b,
    ss, rs, ws, ls,
):
    a = lax.axis_index("dp")
    c = lax.axis_index("expert")
    x, y, k = c // 8, lax.rem(c // 2, 4), lax.rem(c, 2)

    def at(z_, x_, y_, k_):
        return (z_, (x_ * 4 + y_) * 2 + k_)

    def m4(v):
        return lax.rem(v, 4)

    loads = [
        pltpu.make_async_copy(src, dst, ws.at[i])
        for i, (src, dst) in enumerate(
            [(w_out_h, w_out), (sg_h, sg), (su_h, su), (sd_h, sd), (wg_h.at[0], wg), (wu_h.at[0], wu), (wd_h.at[0], wd)]
        )
    ]
    loads[0].start()

    barrier = pltpu.get_barrier_semaphore()
    peers = [at(m4(a + i), x, y, k) for i in (1, 2, 3)]
    peers += [at(a, x, m4(y + i), lax.rem(k + j, 2)) for i in range(4) for j in range(2) if i or j]
    peers += [at(a, m4(x + i), y, lax.rem(k + j, 2)) for i in (1, 2, 3) for j in range(2)]
    for peer in peers:
        pl.semaphore_signal(barrier, inc=1, device_id=peer, device_id_type=MESH)

    sent, finished = [], set()

    def send(i, src, dst, device):
        copy = pltpu.make_async_remote_copy(
            src_ref=src, dst_ref=dst, send_sem=ss.at[i], recv_sem=rs.at[i], device_id=device, device_id_type=MESH
        )
        copy.start()
        sent.append(copy)
        return copy

    zdev = lambda i: at(i, x, y, k)
    xdev = lambda i: at(a, i, y, k)
    ydev = lambda i: at(a, x, i, k)

    def others(me, base, dev, src, dst):
        return [send(base + i - 1, src(m4(me + i)), dst(m4(me + i)), dev(m4(me + i))) for i in (1, 2, 3)]

    def ring(base, buf, me, dev, half=64):
        right, left = m4(me + 1), m4(me + 3)
        top, bottom = pl.ds(0, half), pl.ds(half, half)
        go = lambda i, slot, part, to: send(base + i, buf.at[slot, part], buf.at[slot, part], dev(to))
        copies = [go(0, me, top, right), go(1, me, bottom, left), go(2, me, bottom, right), go(3, me, top, left)]

        def forward():
            copies[0].wait_recv()
            copies.append(go(4, left, top, right))
            copies[1].wait_recv()
            copies.append(go(5, right, bottom, left))

        return copies, forward

    def ring_sum(base, sums, middle, finals, me, dev):
        right, left, far = m4(me + 1), m4(me + 3), m4(me + 2)
        top, bottom = pl.ds(0, 64), pl.ds(64, 64)
        copies = {}

        def go(i, slot, part, landing, to):
            copies[i] = send(base + i, sums.at[slot, part], landing, dev(to))

        def far_ready():
            go(0, far, top, middle.at[0], right)
            go(1, far, bottom, middle.at[1], left)

        def right_ready():
            go(2, right, bottom, finals.at[0, bottom], right)

        def left_ready():
            go(3, left, top, finals.at[1, top], left)

        def pass_on():
            copies[0].wait_recv()
            sums[right, top, :] = (sums[right, top, :].astype(F32) + middle[0].astype(F32)).astype(BF)
            go(4, right, top, finals.at[0, top], right)
            copies[1].wait_recv()
            sums[left, bottom, :] = (sums[left, bottom, :].astype(F32) + middle[1].astype(F32)).astype(BF)
            go(5, left, bottom, finals.at[1, bottom], left)

        def landed():
            for i in (2, 3, 4, 5):
                copies[i].wait_recv()

        return far_ready, right_ready, left_ready, pass_on, landed

    left, right, opposite = m4(a + 3), m4(a + 1), m4(a + 2)
    top, bottom = pl.ds(0, 64), pl.ds(64, 64)
    hid[0:120, :] = pre[...].astype(F32)
    hid[120:128, :] = jnp.zeros((8, 2048), F32)
    zb[0, 0:64, :] = hid[0:64, :].astype(BF)
    for i in range(4):
        held_f[4 * i : 4 * i + 4, :] = held[:, 512 * i : 512 * i + 512].astype(F32)
    held_s[...] = held_f[...].astype(BF)
    held_all[a] = held_s[...]
    loads[0].wait()

    pl.semaphore_wait(barrier, len(peers))

    piece_rows = pl.ds(pl.multiple_of((x * 4 + y) * 128, 128), 128)
    piece_cols = lambda i: pl.ds(pl.multiple_of(k * 256 + i * 128, 128), 128)
    pieces = [send(ID["W_PIECE"], w_out.at[piece_rows, piece_cols(0)], wo_a.at[k, y, x], zdev(opposite))]
    pieces += [send(ID["W_PIECE"] + 1, w_out.at[piece_rows, piece_cols(1)], wo_b.at[k, x, y], zdev(opposite))]
    held_copies = others(a, ID["HELD"], zdev, lambda i: held_s, lambda i: held_all.at[a])

    def both(base, part):
        return [
            send(base, zb.at[0, part], zb.at[1, part], zdev(right)),
            send(base + 1, zb.at[0, part], zb.at[2, part], zdev(left)),
        ]

    tops = both(ID["Z_TOP"], top)
    for load in loads[1:]:
        load.start()

    idsp[...] = jnp.full((8, 128), -1, jnp.int32)
    idsp[0:6, 0:124] = ids[...]
    lane = iota((32, 128), 1)
    row = iota((32, 128), 0)
    alive = (lane < live[0]) | (lane >= 120)
    before = jnp.where(iota((128, 128), 0) < iota((128, 128), 1), 1.0, 0.0).astype(BF)

    def match(expert):
        hit = idsp[0:1, :] == expert
        for i in range(1, 6):
            hit = hit | (idsp[i : i + 1, :] == expert)
        return jnp.where(hit & alive, 1.0, 0.0)

    hits = match(row)
    ranks = dot(hits.astype(BF), before)
    code_a[...] = jnp.where(hits > 0.5, ranks + (24 * x).astype(F32), -1.0)
    hits_b = match(lax.rem(row // 2, 4) * 8 + row // 8 * 2 + lax.rem(row, 2))
    ranks_b = dot(hits_b.astype(BF), before)
    code_b[...] = jnp.where(hits_b > 0.5, ranks_b + (24 * y).astype(F32), -1.0)

    def tile(ref, i):
        return ref.at[pl.ds(pl.multiple_of(i * 8, 8), 8)]

    ca[x] = code_a[pl.ds(pl.multiple_of(x * 8, 8), 8), :]
    cb[y] = code_b[pl.ds(pl.multiple_of(y * 8, 8), 8), :]
    code_copies = others(x, ID["CODE_A"], xdev, lambda i: tile(code_a, i), lambda i: ca.at[x])
    code_copies += others(y, ID["CODE_B"], ydev, lambda i: tile(code_b, i), lambda i: cb.at[y])

    counts = lax.dot_general(jnp.ones((8, 128), BF), hits.astype(BF), NT, preferred_element_type=F32)
    copy_index = iota((8, 32), 0)
    offset = lax.rem(copy_index - pick[...] + 4, 4)
    served = (counts.astype(jnp.int32) - offset + 3) // 4
    svt[...] = jnp.zeros((8, 128), F32)
    svt[:, 0:32] = jnp.where(copy_index < 4, served, 0).astype(F32)
    crz[a] = svt[...]
    cr_copies = others(a, ID["CR_Z"], zdev, lambda i: svt, lambda i: crz.at[a])

    row64, col64 = iota((64, 64), 0), iota((64, 64), 1)
    chosen = jnp.full((64, 64), -64, jnp.int32)
    for i in range(4):
        chosen = jnp.where(row64 == 56 + i, source[i] // 4 * 16 + lax.rem(source[i], 4), chosen)
    for copy in held_copies:
        copy.wait_recv()
    for i in range(4):
        cols = slice(512 * i, 512 * i + 512)
        picked = dot(jnp.where(col64 == chosen + 4 * i, 1.0, 0.0).astype(BF), held_all[...].reshape(64, 512))
        zb[0, 64:128, cols] = (hid[64:128, cols] + picked).astype(BF)
    bottoms = both(ID["Z_BOTTOM"], bottom)
    for copy in pieces:
        copy.wait_recv()
    ax_copies, ax_forward = ring(ID["WA_X"], wo_a.at[k, y], x, xdev)
    by_copies, by_forward = ring(ID["WB_Y"], wo_b.at[k, x], y, ydev)
    pr[a] = dot(zb[0], w_out[...]).astype(BF)
    ax_forward()
    by_forward()
    for copy in ax_copies[2:]:
        copy.wait_recv()
    ay_copies, ay_forward = ring(ID["WA_Y"], wo_a.at[k], y, ydev, 2)
    for copy in by_copies[2:]:
        copy.wait_recv()
    bx_copies, bx_forward = ring(ID["WB_X"], wo_b.at[k], x, xdev, 2)
    ay_forward()
    bx_forward()
    for copy in ay_copies[2:]:
        copy.wait_recv()
    core_copies = [send(ID["W_CORE"], wo_a.at[k], wo_a.at[k], at(a, x, y, 1 - k))]
    for copy in bx_copies[2:]:
        copy.wait_recv()
    core_copies += [send(ID["W_CORE"] + 1, wo_b.at[k], wo_b.at[k], at(a, x, y, 1 - k))]
    returns = []
    for i, slot in enumerate((left, right)):
        tops[i].wait_recv()
        bottoms[i].wait_recv()
        pb[i] = dot(zb[1 + i], w_out[...]).astype(BF)
        returns.append(send(ID["Z_RET"] + i, pb.at[i], pr.at[a], zdev(slot)))
    for copy in core_copies:
        copy.wait_recv()
    far = jnp.zeros((128, 512), F32)
    for i in range(8):
        rows = [
            jnp.concatenate([wo_a[0, n, m], wo_b[0, m, n], wo_a[1, n, m], wo_b[1, m, n]], axis=1)
            for m, n in ((i // 2, i % 2 * 2), (i // 2, i % 2 * 2 + 1))
        ]
        far = far + dot(zb[0, :, 256 * i : 256 * i + 256], jnp.concatenate(rows, axis=0))
    pr[opposite] = far.astype(BF)

    for copy in cr_copies:
        copy.wait_recv()
    crs[0] = crz[0] + crz[1] + crz[2] + crz[3]
    crx[x] = crs[0]
    cr_copies = others(x, ID["CR_X"], xdev, lambda i: crs.at[0], lambda i: crx.at[x])

    hid[120:128, :] = jnp.zeros((8, 2048), F32)
    hid[0:124, :] = resid[...].astype(F32)
    for copy in returns:
        copy.wait_recv()
    for i in range(4):
        cols = slice(i * 512, i * 512 + 512)
        hid[:, cols] = hid[:, cols] + pr[i].astype(F32)

    def norm(i, _):
        rows = pl.ds(pl.multiple_of(i * 16, 16), 16)
        v = hid[rows, :]
        scale = lax.rsqrt(jnp.mean(v * v, axis=1, keepdims=True) + EPSILON)
        normed = (v * scale * gain[...]).astype(BF)
        buf_a[x, rows, :] = normed[:, 0:1024]
        buf_b[y, rows, :] = normed[:, 1024:2048]
        sb[a, rows, :] = normed
        return 0

    lax.fori_loop(0, 8, norm, 0)
    x_copies, x_forward = ring(ID["X_AG"], buf_a, x, xdev)
    y_copies, y_forward = ring(ID["Y_AG"], buf_b, y, ydev)
    s_copies, s_forward = ring(ID["S_AG"], sb, a, zdev)

    logits = lax.dot_general(router_t[...], sb[a], NT, preferred_element_type=F32)
    powers = jnp.exp(logits - jnp.max(logits, axis=0, keepdims=True))
    prob_a[...] = powers / jnp.sum(powers, axis=0, keepdims=True)
    for i in range(16):
        j = i % 4 * 4 + i // 4
        prob_b[2 * i : 2 * i + 2, :] = prob_a[2 * j : 2 * j + 2, :]
    pa[x] = prob_a[pl.ds(pl.multiple_of(x * 8, 8), 8), :]
    pb_b[y] = prob_b[pl.ds(pl.multiple_of(y * 8, 8), 8), :]
    prob_copies = others(x, ID["PROB_A"], xdev, lambda i: tile(prob_a, i), lambda i: pa.at[x])
    prob_copies += others(y, ID["PROB_B"], ydev, lambda i: tile(prob_b, i), lambda i: pb_b.at[y])

    x_forward()
    y_forward()
    s_forward()
    for copy in cr_copies:
        copy.wait_recv()
    crs[1] = crx[0] + crx[1] + crx[2] + crx[3]
    cry[y] = crs[1]
    cr_copies = others(y, ID["CR_Y"], ydev, lambda i: crs.at[1], lambda i: cry.at[y])
    for copy in code_copies:
        copy.wait_recv()

    slot96 = iota((96, 512), 0).astype(F32)

    def codes(ref, i):
        return jnp.concatenate([ref[s, pl.ds(i, 1), :] for s in range(4)], axis=1)

    locals_ = []

    def dispatch(base, step, core, code, buf, slots, landing, me, dev, group):
        for i in range(4):
            onehot[96 * i : 96 * i + 96, :] = jnp.where(slot96 == codes(code, 2 * i + core), 1.0, 0.0).astype(BF)

        def columns(n, _):
            cols = pl.ds(pl.multiple_of(n * 256, 256), 256)
            rows = buf[:, :, cols].reshape(512, 256)
            slots[core, :, :, cols] = dot(onehot[...], rows).astype(BF).reshape(4, 96, 256)
            return 0

        lax.fori_loop(0, 4, columns, 0, unroll=True)
        copies = []
        for i in range(4):
            to = m4(me + i)
            if step == 0 and i == 0:
                copy = pltpu.make_async_copy(slots.at[core, to], landing.at[k, me], ls.at[base])
                copy.start()
                locals_.append(copy)
                continue
            copies.append(send(group + 4 * step + i, slots.at[core, to], landing.at[k, me], dev(to, core)))
        return copies

    col_dev = lambda i, core: at(a, x, i, core)
    row_dev = lambda i, core: at(a, i, y, core)
    for copy in x_copies[2:]:
        copy.wait_recv()
    arrive = [[], []]
    arrive[0] += dispatch(0, 0, k, ca, buf_a, s2a, r2a, y, col_dev, ID["DIS_A"])
    for copy in y_copies[2:]:
        copy.wait_recv()
    arrive[0] += dispatch(1, 0, k, cb, buf_b, s2b, r2b, x, row_dev, ID["DIS_B"])
    arrive[1] += dispatch(0, 1, 1 - k, ca, buf_a, s2a, r2a, y, col_dev, ID["DIS_A"])
    arrive[1] += dispatch(1, 1, 1 - k, cb, buf_b, s2b, r2b, x, row_dev, ID["DIS_B"])

    for load in loads[1:4]:
        load.wait()

    def shared(i):
        rows = sb[i]
        gate = lax.dot_general(rows, sg[...], NT, preferred_element_type=F32)
        up = lax.dot_general(rows, su[...], NT, preferred_element_type=F32)
        hidden_units = (gate / (1.0 + jnp.exp(-gate)) * up).astype(BF)

        def columns(n, _):
            cols = pl.ds(pl.multiple_of(n * 512, 512), 512)
            sp[i, :, cols] = dot(hidden_units, sd[:, cols]).astype(BF)
            return 0

        lax.fori_loop(0, 4, columns, 0, unroll=True)

    def shared_of(i, parts):
        for part in parts:
            s_copies[part].wait_recv()
        shared(m4(a + i))

    s_far, s_right, s_left, s_pass, s_landed = ring_sum(ID["S_SUM"], sp, s_mid, sr, a, zdev)
    shared(a)
    shared_of(3, (2,))
    s_left()
    shared_of(1, (3,))
    s_right()

    for copy in prob_copies:
        copy.wait_recv()

    def weights(code, prob, into):
        for i in range(8):
            e = lax.rem(i, 4) * 2 + i // 4
            hit = slot96 == codes(code, e)
            wide[96 * i : 96 * i + 96, :] = jnp.where(hit, codes(prob, e), 0.0)
        into[...] = wide[...].T.astype(BF)

    weights(ca, pa, wca)
    weights(cb, pb_b, wcb)

    for copy in cr_copies:
        copy.wait_recv()
    crs[2] = cry[0] + cry[1] + cry[2] + cry[3]
    crk[k] = crs[2]
    cr_copy = send(ID["CR_K"], crs.at[2], crk.at[k], at(a, x, y, 1 - k))

    for load in loads[4:]:
        load.wait()

    def swapped(v):
        return jnp.concatenate([v[(j * 4 + i) * 24 : (j * 4 + i) * 24 + 24] for i in range(4) for j in range(4)], axis=0)

    def expert(step, core):
        for copy in arrive[step]:
            copy.wait_recv()
        if step == 0:
            for copy in locals_:
                copy.wait()

        def up(cols):
            first = jnp.concatenate([wg[0:1024, cols], wu[0:1024, cols]], axis=1)
            second = jnp.concatenate([wg[1024:2048, cols], wu[1024:2048, cols]], axis=1)
            h = dot(r2a[core].reshape(384, 1024), first) + swapped(dot(r2b[core].reshape(384, 1024), second))
            width = h.shape[1] // 2
            gate = h[:, 0:width]
            inner = gate / (1.0 + jnp.exp(-gate)) * h[:, width : 2 * width]
            inner_a[:, cols] = inner.astype(BF)
            inner_b[:, cols] = swapped(inner).astype(BF)

        for first in range(0, 1408, 256):
            up(slice(first, min(first + 256, 1408)))
        for copy in arrive[step]:
            copy.wait_send()
            finished.add(id(copy))
        copies = []
        for group, inner, slots, landing, me, dev, first in (
            (ID["RET_A"], inner_a, s2a, r3a, y, col_dev, 0),
            (ID["RET_B"], inner_b, s2b, r3b, x, row_dev, 1024),
        ):

            for n in (0, 512):
                out_cols = dot(inner[...], wd[:, first + n : first + n + 512])
                slots[core, :, :, n : n + 512] = out_cols.astype(BF).reshape(4, 96, 512)
            for i in range(4):
                to = m4(me + i)
                if step == 0 and i == 0:
                    copy = pltpu.make_async_copy(slots.at[core, to], landing.at[k, me], ls.at[2 + (group == ID["RET_B"])])
                    copy.start()
                    locals_.append(copy)
                    continue
                copies.append(send(group + 4 * step + i, slots.at[core, to], landing.at[k, me], dev(to, core)))
        return copies

    back = expert(0, k)
    shared_of(2, (4, 5))
    s_far()
    back += expert(1, 1 - k)
    s_pass()
    back_a, back_b = [back[i] for i in (0, 1, 2, 6, 7, 8, 9)], [back[i] for i in (3, 4, 5, 10, 11, 12, 13)]

    def combine(wc, landed, sums, i):
        rows = pl.ds(pl.multiple_of(i * 128, 128), 128)
        sums[i] = dot(wc[rows, :], landed[...].reshape(768, 1024)).astype(BF)

    a_far, a_right, a_left, a_pass, a_landed = ring_sum(ID["SUM_A"], s4a, mid_a, r4a, x, xdev)
    b_far, b_right, b_left, b_pass, b_landed = ring_sum(ID["SUM_B"], s4b, mid_b, r4b, y, ydev)
    for copies, local, part, me, ready in ((back_a, locals_[2], (wca, r3a, s4a), x, a_far), (back_b, locals_[3], (wcb, r3b, s4b), y, b_far)):
        for copy in copies:
            copy.wait_recv()
        local.wait()
        combine(*part, m4(me + 2))
        ready()
    for part, me, rest in (((wca, r3a, s4a), x, (a_right, a_left)), ((wcb, r3b, s4b), y, (b_right, b_left))):
        combine(*part, m4(me + 1))
        rest[0]()
        combine(*part, m4(me + 3))
        rest[1]()
    a_pass()
    b_pass()
    combine(wca, r3a, s4a, x)
    combine(wcb, r3b, s4b, y)

    cr_copy.wait_recv()
    served_all = crk[0] + crk[1]
    mine = (iota((8, 128), 0) == a) & (iota((8, 128), 1) == c)
    copy_rows[0] = jnp.sum(jnp.where(mine, served_all, 0.0)).astype(jnp.int32)

    s_landed()
    for landed, own, finals, me, first in ((a_landed, s4a, r4a, x, 0), (b_landed, s4b, r4b, y, 1024)):
        landed()

        def total(n, _):
            cols = pl.ds(pl.multiple_of(n * 256, 256), 256)
            wide_cols = pl.ds(pl.multiple_of(first + n * 256, 256), 256)
            v = hid[:, wide_cols] + sp[a, :, wide_cols].astype(F32) + own[me, :, cols].astype(F32)
            for i in range(2):
                v = v + sr[i, :, wide_cols].astype(F32) + finals[i, :, cols].astype(F32)
            out[:, wide_cols] = v[0:124].astype(BF)
            return 0

        lax.fori_loop(0, 4, total, 0)
    for copy in sent:
        if id(copy) not in finished:
            copy.wait_send()


def body(
    attn_prefill, decode_held, decode_source, residual, live_rows, expert_ids, replica_pick, w_out, norm_gain, router,
    exp_gate, exp_up, exp_down, shared_gate, shared_up, shared_down,
):
    vmem = pl.BlockSpec(memory_space=pltpu.VMEM)
    smem = pl.BlockSpec(memory_space=pltpu.SMEM)
    hbm = pl.BlockSpec(memory_space=pl.ANY)
    V = pltpu.VMEM
    return pl.pallas_call(
        kernel,
        out_shape=(jax.ShapeDtypeStruct((124, 2048), BF), jax.ShapeDtypeStruct((1,), jnp.int32)),
        in_specs=[vmem, vmem, smem, vmem, smem, vmem, vmem, hbm, vmem, vmem, hbm, hbm, hbm, hbm, hbm, hbm],
        out_specs=(vmem, smem),
        scratch_shapes=[
            V((2048, 512), BF), V((2048, 1408), BF), V((2048, 1408), BF), V((1408, 2048), BF),
            V((352, 2048), BF), V((352, 2048), BF), V((352, 2048), BF),
            V((128, 2048), F32), V((3, 128, 2048), BF), V((2, 128, 512), BF), V((4, 128, 512), BF),
            V((16, 512), F32), V((16, 512), BF), V((4, 16, 512), BF),
            V((2, 4, 4, 128, 128), BF), V((2, 4, 4, 128, 128), BF),
            V((8, 128), jnp.int32), V((32, 128), F32), V((32, 128), F32), V((4, 8, 128), F32), V((4, 8, 128), F32),
            V((8, 128), F32), V((4, 8, 128), F32), V((4, 8, 128), F32), V((4, 8, 128), F32), V((2, 8, 128), F32),
            V((3, 8, 128), F32),
            V((32, 128), F32), V((32, 128), F32), V((4, 8, 128), F32), V((4, 8, 128), F32),
            V((4, 128, 1024), BF), V((4, 128, 1024), BF),
            V((4, 128, 2048), BF), V((4, 128, 2048), BF), V((2, 64, 2048), BF), V((2, 128, 2048), BF),
            V((384, 512), BF),
            V((2, 4, 96, 1024), BF), V((2, 4, 96, 1024), BF), V((2, 4, 96, 1024), BF), V((2, 4, 96, 1024), BF),
            V((384, 1408), BF), V((384, 1408), BF),
            V((2, 4, 96, 1024), BF), V((2, 4, 96, 1024), BF),
            V((768, 512), F32), V((512, 768), BF), V((512, 768), BF),
            V((4, 128, 1024), BF), V((4, 128, 1024), BF), V((2, 64, 1024), BF), V((2, 64, 1024), BF),
            V((2, 128, 1024), BF), V((2, 128, 1024), BF),
            pltpu.SemaphoreType.DMA((COPIES,)), pltpu.SemaphoreType.DMA((COPIES,)),
            pltpu.SemaphoreType.DMA((7,)), pltpu.SemaphoreType.DMA((4,)),
        ],
        compiler_params=pltpu.CompilerParams(collective_id=0, has_side_effects=True, vmem_limit_bytes=62 << 20),
        cost_estimate=pl.CostEstimate(flops=17_000_000_000, bytes_accessed=26_000_000, transcendentals=2_000_000),
        name="moe",
    )(
        attn_prefill, decode_held, decode_source, residual, live_rows, expert_ids.T, replica_pick, w_out,
        norm_gain.reshape(1, 2048), router.T, exp_gate, exp_up, exp_down, shared_gate, shared_up, shared_down,
    )


def solution(mesh):
    rows = P(("dp", "expert"), None)
    flat = P(("dp", "expert"))
    placed = (
        rows, rows, flat, rows, flat, rows, rows, P(None, "dp"), P(), P(),
        P("expert", None, None), P("expert", None, None), P("expert", None, None),
        P("dp", None), P("dp", None), P("dp", None),
    )
    return jax.shard_map(body, mesh=mesh, in_specs=placed, out_specs=(rows, flat), check_vma=False)
```

```python
import functools

import jax
import jax.numpy as jnp
from jax import lax
from jax.experimental import pallas as pl
from jax.experimental.pallas import tpu as pltpu
from jax.sharding import PartitionSpec as P

EPSILON = 1e-06
MESH = pl.DeviceIdType.MESH
BF = jnp.bfloat16
F32 = jnp.float32
NT = (((1,), (1,)), ((), ()))

GROUPS = dict(
    Z_TOP=2, Z_BOTTOM=2, Z_RET=4, HELD=3, W_PIECE=2, WA_X=3, WA_Y=3, WB_Y=3, WB_X=3, W_CORE=8, CODE_A=3, CODE_B=3, CR_Z=3,
    CR_X=3, CR_Y=3, CR_K=1, PROB_A=3, PROB_B=3, X_AG=6, Y_AG=6, S_AG=6, DIS_A=8, DIS_B=8, S_SUM=6, RET_A=8, RET_B=8, SUM_A=6, SUM_B=6,
)
COPIES = sum(GROUPS.values())
ID = {name: sum(list(GROUPS.values())[:i]) for i, name in enumerate(GROUPS)}


def dot(a, b):
    return jnp.dot(a, b, preferred_element_type=F32)


def iota(shape, dim):
    return lax.broadcasted_iota(jnp.int32, shape, dim)


def kernel(
    pre, held, source, resid, live, ids, pick, w_out_h, gain, router_t, wg_h, wu_h, wd_h, sg_h, su_h, sd_h,
    out, copy_rows,
    w_out, wg, wu, wd, sg, su, sd,
    hid, zb, pb, pr, held_f, held_s, held_all, wo_a, wo_b, idsp, code_a, code_b, ca, cb, svt, crz, crx, cry, crk, crs,
    prob_a, prob_b, pa, pb_b, buf_a, buf_b, sb, sp, s_mid, sr, onehot, s2a, s2b, r2a, r2b, inner_a, inner_b,
    r3a, r3b, wide, wca, wcb, s4a, s4b, mid_a, mid_b, r4a, r4b,
    ss, rs, ws, ls,
):
    a = lax.axis_index("dp")
    c = lax.axis_index("expert")
    x, y, k = c // 8, lax.rem(c // 2, 4), lax.rem(c, 2)

    def at(z_, x_, y_, k_):
        return (z_, (x_ * 4 + y_) * 2 + k_)

    def m4(v):
        return lax.rem(v, 4)

    loads = [
        pltpu.make_async_copy(src, dst, ws.at[i])
        for i, (src, dst) in enumerate(
            [(w_out_h, w_out), (sg_h, sg), (su_h, su), (sd_h, sd), (wg_h.at[0], wg), (wu_h.at[0], wu), (wd_h.at[0], wd)]
        )
    ]
    loads[0].start()

    barrier = pltpu.get_barrier_semaphore()
    peers = [at(m4(a + i), x, y, k) for i in (1, 2, 3)]
    peers += [at(a, x, m4(y + i), lax.rem(k + j, 2)) for i in range(4) for j in range(2) if i or j]
    peers += [at(a, m4(x + i), y, lax.rem(k + j, 2)) for i in (1, 2, 3) for j in range(2)]
    for peer in peers:
        pl.semaphore_signal(barrier, inc=1, device_id=peer, device_id_type=MESH)

    sent, finished = [], set()

    def send(i, src, dst, device):
        copy = pltpu.make_async_remote_copy(
            src_ref=src, dst_ref=dst, send_sem=ss.at[i], recv_sem=rs.at[i], device_id=device, device_id_type=MESH
        )
        copy.start()
        sent.append(copy)
        return copy

    zdev = lambda i: at(i, x, y, k)
    xdev = lambda i: at(a, i, y, k)
    ydev = lambda i: at(a, x, i, k)

    def others(me, base, dev, src, dst):
        return [send(base + i - 1, src(m4(me + i)), dst(m4(me + i)), dev(m4(me + i))) for i in (1, 2, 3)]

    def ring(base, buf, me, dev, half=64):
        right, left = m4(me + 1), m4(me + 3)
        top, bottom = pl.ds(0, half), pl.ds(half, half)
        go = lambda i, slot, part, to: send(base + i, buf.at[slot, part], buf.at[slot, part], dev(to))
        copies = [go(0, me, top, right), go(1, me, bottom, left), go(2, me, bottom, right), go(3, me, top, left)]

        def forward():
            copies[0].wait_recv()
            copies.append(go(4, left, top, right))
            copies[1].wait_recv()
            copies.append(go(5, right, bottom, left))

        return copies, forward

    def ring_sum(base, sums, middle, finals, me, dev):
        right, left, far = m4(me + 1), m4(me + 3), m4(me + 2)
        top, bottom = pl.ds(0, 64), pl.ds(64, 64)
        copies = {}

        def go(i, slot, part, landing, to):
            copies[i] = send(base + i, sums.at[slot, part], landing, dev(to))

        def far_ready():
            go(0, far, top, middle.at[0], right)
            go(1, far, bottom, middle.at[1], left)

        def right_ready():
            go(2, right, bottom, finals.at[0, bottom], right)

        def left_ready():
            go(3, left, top, finals.at[1, top], left)

        def pass_on():
            copies[0].wait_recv()
            sums[right, top, :] = (sums[right, top, :].astype(F32) + middle[0].astype(F32)).astype(BF)
            go(4, right, top, finals.at[0, top], right)
            copies[1].wait_recv()
            sums[left, bottom, :] = (sums[left, bottom, :].astype(F32) + middle[1].astype(F32)).astype(BF)
            go(5, left, bottom, finals.at[1, bottom], left)

        def landed():
            for i in (2, 3, 4, 5):
                copies[i].wait_recv()

        return far_ready, right_ready, left_ready, pass_on, landed

    left, right, opposite = m4(a + 3), m4(a + 1), m4(a + 2)
    top, bottom = pl.ds(0, 64), pl.ds(64, 64)
    hid[0:120, :] = pre[...].astype(F32)
    hid[120:128, :] = jnp.zeros((8, 2048), F32)
    zb[0, 0:64, :] = hid[0:64, :].astype(BF)
    for i in range(4):
        held_f[4 * i : 4 * i + 4, :] = held[:, 512 * i : 512 * i + 512].astype(F32)
    held_s[...] = held_f[...].astype(BF)
    held_all[a] = held_s[...]
    loads[0].wait()

    pl.semaphore_wait(barrier, len(peers))

    piece_rows = pl.ds(pl.multiple_of((x * 4 + y) * 128, 128), 128)
    piece_cols = lambda i: pl.ds(pl.multiple_of(k * 256 + i * 128, 128), 128)
    pieces = [send(ID["W_PIECE"], w_out.at[piece_rows, piece_cols(0)], wo_a.at[k, y, x], zdev(opposite))]
    pieces += [send(ID["W_PIECE"] + 1, w_out.at[piece_rows, piece_cols(1)], wo_b.at[k, x, y], zdev(opposite))]
    held_copies = others(a, ID["HELD"], zdev, lambda i: held_s, lambda i: held_all.at[a])

    def both(base, part):
        return [
            send(base, zb.at[0, part], zb.at[1, part], zdev(right)),
            send(base + 1, zb.at[0, part], zb.at[2, part], zdev(left)),
        ]

    tops = both(ID["Z_TOP"], top)
    for load in loads[1:]:
        load.start()

    row64, col64 = iota((64, 64), 0), iota((64, 64), 1)
    chosen = jnp.full((64, 64), -64, jnp.int32)
    for i in range(4):
        chosen = jnp.where(row64 == 56 + i, source[i] // 4 * 16 + lax.rem(source[i], 4), chosen)
    for copy in pieces:
        copy.wait_recv()
    ax_copies = others(x, ID["WA_X"], xdev, lambda i: wo_a.at[k, y, x], lambda i: wo_a.at[k, y, x])
    by_copies = others(y, ID["WB_Y"], ydev, lambda i: wo_b.at[k, x, y], lambda i: wo_b.at[k, x, y])
    for copy in held_copies:
        copy.wait_recv()
    for i in range(4):
        cols = slice(512 * i, 512 * i + 512)
        picked = dot(jnp.where(col64 == chosen + 4 * i, 1.0, 0.0).astype(BF), held_all[...].reshape(64, 512))
        zb[0, 64:128, cols] = (hid[64:128, cols] + picked).astype(BF)
    bottoms = both(ID["Z_BOTTOM"], bottom)
    for copy in ax_copies:
        copy.wait_recv()
    ay_copies = others(y, ID["WA_Y"], ydev, lambda i: wo_a.at[k, y], lambda i: wo_a.at[k, y])
    for copy in by_copies:
        copy.wait_recv()
    bx_copies = others(x, ID["WB_X"], xdev, lambda i: wo_b.at[k, x], lambda i: wo_b.at[k, x])

    def to_sibling(i, wo, slot):
        return send(ID["W_CORE"] + i, wo.at[k, slot], wo.at[k, slot], at(a, x, y, 1 - k))

    core_copies = [to_sibling(0, wo_a, y), to_sibling(4, wo_b, x)]

    idsp[...] = jnp.full((8, 128), -1, jnp.int32)
    idsp[0:6, 0:124] = ids[...]
    lane = iota((32, 128), 1)
    row = iota((32, 128), 0)
    alive = (lane < live[...]) | (lane >= 120)
    before = jnp.where(iota((128, 128), 0) < iota((128, 128), 1), 1.0, 0.0).astype(BF)

    def match(expert):
        hit = idsp[0:1, :] == expert
        for i in range(1, 6):
            hit = hit | (idsp[i : i + 1, :] == expert)
        return jnp.where(hit & alive, 1.0, 0.0)

    hits = match(row)
    ranks = dot(hits.astype(BF), before)
    code_a[...] = jnp.where(hits > 0.5, ranks + (24 * x).astype(F32), -1.0)
    hits_b = match(lax.rem(row // 2, 4) * 8 + row // 8 * 2 + lax.rem(row, 2))
    ranks_b = dot(hits_b.astype(BF), before)
    code_b[...] = jnp.where(hits_b > 0.5, ranks_b + (24 * y).astype(F32), -1.0)

    def tile(ref, i):
        return ref.at[pl.ds(pl.multiple_of(i * 8, 8), 8)]

    ca[x] = code_a[pl.ds(pl.multiple_of(x * 8, 8), 8), :]
    cb[y] = code_b[pl.ds(pl.multiple_of(y * 8, 8), 8), :]
    code_copies = others(x, ID["CODE_A"], xdev, lambda i: tile(code_a, i), lambda i: ca.at[x])
    code_copies += others(y, ID["CODE_B"], ydev, lambda i: tile(code_b, i), lambda i: cb.at[y])

    counts = lax.dot_general(jnp.ones((8, 128), BF), hits.astype(BF), NT, preferred_element_type=F32)
    copy_index = iota((8, 32), 0)
    offset = lax.rem(copy_index - pick[...] + 4, 4)
    served = (counts.astype(jnp.int32) - offset + 3) // 4
    svt[...] = jnp.zeros((8, 128), F32)
    svt[:, 0:32] = jnp.where(copy_index < 4, served, 0).astype(F32)
    crz[a] = svt[...]
    cr_copies = others(a, ID["CR_Z"], zdev, lambda i: svt, lambda i: crz.at[a])

    pr[a] = dot(zb[0], w_out[...]).astype(BF)
    returns = []

    def project(i, copies, part):
        for copy in copies:
            copy.wait_recv()
        rows = jnp.concatenate([zb[1, part, :], zb[2, part, :]], axis=0)
        pb[i] = dot(rows, w_out[...]).astype(BF)
        returns.append(send(ID["Z_RET"] + 2 * i, pb.at[i, top], pr.at[a, part], zdev(left)))
        returns.append(send(ID["Z_RET"] + 2 * i + 1, pb.at[i, bottom], pr.at[a, part], zdev(right)))

    project(0, tops, top)
    for i in (1, 2, 3):
        ay_copies[i - 1].wait_recv()
        core_copies.append(to_sibling(i, wo_a, m4(y + 4 - i)))
        bx_copies[i - 1].wait_recv()
        core_copies.append(to_sibling(4 + i, wo_b, m4(x + 4 - i)))
    project(1, bottoms, bottom)

    def far(core):
        v = jnp.zeros((128, 256), F32)
        for i in range(8):
            m, n = i // 2, i % 2 * 2
            rows = [jnp.concatenate([wo_a[core, j, m], wo_b[core, m, j]], axis=1) for j in (n, n + 1)]
            v = v + dot(zb[0, :, 256 * i : 256 * i + 256], jnp.concatenate(rows, axis=0))
        pr[opposite, :, pl.ds(pl.multiple_of(core * 256, 256), 256)] = v.astype(BF)

    far(k)
    for copy in core_copies:
        copy.wait_recv()
    far(1 - k)

    for copy in cr_copies:
        copy.wait_recv()
    crs[0] = crz[0] + crz[1] + crz[2] + crz[3]
    crx[x] = crs[0]
    cr_copies = others(x, ID["CR_X"], xdev, lambda i: crs.at[0], lambda i: crx.at[x])

    hid[120:128, :] = jnp.zeros((8, 2048), F32)
    hid[0:124, :] = resid[...].astype(F32)
    for copy in returns:
        copy.wait_recv()
    for i in range(4):
        cols = slice(i * 512, i * 512 + 512)
        hid[:, cols] = hid[:, cols] + pr[i].astype(F32)

    def norm(i, _):
        rows = pl.ds(pl.multiple_of(i * 16, 16), 16)
        v = hid[rows, :]
        scale = lax.rsqrt(jnp.mean(v * v, axis=1, keepdims=True) + EPSILON)
        normed = (v * scale * gain[...]).astype(BF)
        buf_a[x, rows, :] = normed[:, 0:1024]
        buf_b[y, rows, :] = normed[:, 1024:2048]
        sb[a, rows, :] = normed
        return 0

    lax.fori_loop(0, 8, norm, 0)
    x_copies, x_forward = ring(ID["X_AG"], buf_a, x, xdev)
    y_copies, y_forward = ring(ID["Y_AG"], buf_b, y, ydev)
    s_copies, s_forward = ring(ID["S_AG"], sb, a, zdev)

    logits = lax.dot_general(router_t[...], sb[a], NT, preferred_element_type=F32)
    powers = jnp.exp(logits - jnp.max(logits, axis=0, keepdims=True))
    prob_a[...] = powers / jnp.sum(powers, axis=0, keepdims=True)
    for i in range(16):
        j = i % 4 * 4 + i // 4
        prob_b[2 * i : 2 * i + 2, :] = prob_a[2 * j : 2 * j + 2, :]
    pa[x] = prob_a[pl.ds(pl.multiple_of(x * 8, 8), 8), :]
    pb_b[y] = prob_b[pl.ds(pl.multiple_of(y * 8, 8), 8), :]
    prob_copies = others(x, ID["PROB_A"], xdev, lambda i: tile(prob_a, i), lambda i: pa.at[x])
    prob_copies += others(y, ID["PROB_B"], ydev, lambda i: tile(prob_b, i), lambda i: pb_b.at[y])

    x_forward()
    y_forward()
    s_forward()
    for copy in cr_copies:
        copy.wait_recv()
    crs[1] = crx[0] + crx[1] + crx[2] + crx[3]
    cry[y] = crs[1]
    cr_copies = others(y, ID["CR_Y"], ydev, lambda i: crs.at[1], lambda i: cry.at[y])
    for copy in code_copies:
        copy.wait_recv()

    for load in loads[1:4]:
        load.wait()

    def shared(i):
        rows = sb[i]
        gate = lax.dot_general(rows, sg[...], NT, preferred_element_type=F32)
        up = lax.dot_general(rows, su[...], NT, preferred_element_type=F32)
        hidden_units = (gate / (1.0 + jnp.exp(-gate)) * up).astype(BF)

        def columns(n, _):
            cols = pl.ds(pl.multiple_of(n * 512, 512), 512)
            sp[i, :, cols] = dot(hidden_units, sd[:, cols]).astype(BF)
            return 0

        lax.fori_loop(0, 4, columns, 0, unroll=True)

    def shared_of(i, parts):
        for part in parts:
            s_copies[part].wait_recv()
        shared(m4(a + i))

    s_far, s_right, s_left, s_pass, s_landed = ring_sum(ID["S_SUM"], sp, s_mid, sr, a, zdev)
    shared(a)

    slot96 = iota((96, 512), 0).astype(F32)

    def codes(ref, i):
        return jnp.concatenate([ref[s, pl.ds(i, 1), :] for s in range(4)], axis=1)

    locals_ = []

    def dispatch(base, step, core, code, buf, slots, landing, me, dev, group):
        for i in range(4):
            onehot[96 * i : 96 * i + 96, :] = jnp.where(slot96 == codes(code, 2 * i + core), 1.0, 0.0).astype(BF)

        def columns(n, _):
            cols = pl.ds(pl.multiple_of(n * 256, 256), 256)
            rows = buf[:, :, cols].reshape(512, 256)
            slots[core, :, :, cols] = dot(onehot[...], rows).astype(BF).reshape(4, 96, 256)
            return 0

        lax.fori_loop(0, 4, columns, 0, unroll=True)

        def start(i):
            to = m4(me + i)
            if step == 0 and i == 0:
                copy = pltpu.make_async_copy(slots.at[core, to], landing.at[k, me], ls.at[base])
                copy.start()
                locals_.append(copy)
            else:
                arrive[step].append(send(group + 4 * step + i, slots.at[core, to], landing.at[k, me], dev(to, core)))

        return start

    col_dev = lambda i, core: at(a, x, i, core)
    row_dev = lambda i, core: at(a, i, y, core)
    for copy in x_copies[2:]:
        copy.wait_recv()
    arrive = [[], []]
    first_a = dispatch(0, 0, k, ca, buf_a, s2a, r2a, y, col_dev, ID["DIS_A"])
    for i in range(4):
        first_a(i)
    for copy in y_copies[2:]:
        copy.wait_recv()
    first_b = dispatch(1, 0, k, cb, buf_b, s2b, r2b, x, row_dev, ID["DIS_B"])
    for i in range(4):
        first_b(i)
    second_a = dispatch(0, 1, 1 - k, ca, buf_a, s2a, r2a, y, col_dev, ID["DIS_A"])
    second_b = dispatch(1, 1, 1 - k, cb, buf_b, s2b, r2b, x, row_dev, ID["DIS_B"])
    second_a(0)
    second_b(0)

    shared_of(3, (2,))
    s_left()
    shared_of(1, (3,))
    s_right()

    for i in (1, 2, 3):
        for copy, second in ((arrive[0][i - 1], second_a), (arrive[0][i + 2], second_b)):
            copy.wait_send()
            finished.add(id(copy))
            second(i)

    for copy in cr_copies:
        copy.wait_recv()
    crs[2] = cry[0] + cry[1] + cry[2] + cry[3]
    crk[k] = crs[2]
    cr_copy = send(ID["CR_K"], crs.at[2], crk.at[k], at(a, x, y, 1 - k))

    for load in loads[4:]:
        load.wait()

    def swapped(v):
        return jnp.concatenate([v[(j * 4 + i) * 24 : (j * 4 + i) * 24 + 24] for i in range(4) for j in range(4)], axis=0)

    def expert(step, core):
        for copy in arrive[step]:
            copy.wait_recv()
        if step == 0:
            for copy in locals_:
                copy.wait()

        def up(cols):
            first = jnp.concatenate([wg[0:1024, cols], wu[0:1024, cols]], axis=1)
            second = jnp.concatenate([wg[1024:2048, cols], wu[1024:2048, cols]], axis=1)
            h = dot(r2a[core].reshape(384, 1024), first) + swapped(dot(r2b[core].reshape(384, 1024), second))
            width = h.shape[1] // 2
            gate = h[:, 0:width]
            inner = gate / (1.0 + jnp.exp(-gate)) * h[:, width : 2 * width]
            inner_a[:, cols] = inner.astype(BF)
            inner_b[:, cols] = swapped(inner).astype(BF)

        for first in range(0, 1408, 256):
            up(slice(first, min(first + 256, 1408)))
        for copy in arrive[step]:
            if id(copy) not in finished:
                copy.wait_send()
                finished.add(id(copy))
        copies = []
        for group, inner, slots, landing, me, dev, first in (
            (ID["RET_A"], inner_a, s2a, r3a, y, col_dev, 0),
            (ID["RET_B"], inner_b, s2b, r3b, x, row_dev, 1024),
        ):

            for n in (0, 512):
                out_cols = dot(inner[...], wd[:, first + n : first + n + 512])
                slots[core, :, :, n : n + 512] = out_cols.astype(BF).reshape(4, 96, 512)
            for i in range(4):
                to = m4(me + i)
                if step == 0 and i == 0:
                    copy = pltpu.make_async_copy(slots.at[core, to], landing.at[k, me], ls.at[2 + (group == ID["RET_B"])])
                    copy.start()
                    locals_.append(copy)
                    continue
                copies.append(send(group + 4 * step + i, slots.at[core, to], landing.at[k, me], dev(to, core)))
        return copies

    back = expert(0, k)
    back += expert(1, 1 - k)
    shared_of(2, (4, 5))
    s_far()
    back_a, back_b = [back[i] for i in (0, 1, 2, 6, 7, 8, 9)], [back[i] for i in (3, 4, 5, 10, 11, 12, 13)]

    for copy in prob_copies:
        copy.wait_recv()

    def weights(code, prob, into):
        for i in range(8):
            e = lax.rem(i, 4) * 2 + i // 4
            hit = slot96 == codes(code, e)
            wide[96 * i : 96 * i + 96, :] = jnp.where(hit, codes(prob, e), 0.0)
        into[...] = wide[...].T.astype(BF)

    weights(ca, pa, wca)
    weights(cb, pb_b, wcb)

    s_pass()

    def combine(wc, landed, sums, i):
        rows = pl.ds(pl.multiple_of(i * 128, 128), 128)
        sums[i] = dot(wc[rows, :], landed[...].reshape(768, 1024)).astype(BF)

    a_far, a_right, a_left, a_pass, a_landed = ring_sum(ID["SUM_A"], s4a, mid_a, r4a, x, xdev)
    b_far, b_right, b_left, b_pass, b_landed = ring_sum(ID["SUM_B"], s4b, mid_b, r4b, y, ydev)
    for copies, local, part, me, ready in ((back_a, locals_[2], (wca, r3a, s4a), x, a_far), (back_b, locals_[3], (wcb, r3b, s4b), y, b_far)):
        for copy in copies:
            copy.wait_recv()
        local.wait()
        combine(*part, m4(me + 2))
        ready()
    for part, me, rest in (((wca, r3a, s4a), x, (a_right, a_left)), ((wcb, r3b, s4b), y, (b_right, b_left))):
        combine(*part, m4(me + 1))
        rest[0]()
        combine(*part, m4(me + 3))
        rest[1]()
    a_pass()
    b_pass()
    combine(wca, r3a, s4a, x)
    combine(wcb, r3b, s4b, y)

    cr_copy.wait_recv()
    served_all = crk[0] + crk[1]
    mine = (iota((8, 128), 0) == a) & (iota((8, 128), 1) == c)
    copy_rows[0] = jnp.sum(jnp.where(mine, served_all, 0.0)).astype(jnp.int32)

    s_landed()
    for landed, own, finals, me, first in ((a_landed, s4a, r4a, x, 0), (b_landed, s4b, r4b, y, 1024)):
        landed()

        def total(n, _):
            cols = pl.ds(pl.multiple_of(n * 256, 256), 256)
            wide_cols = pl.ds(pl.multiple_of(first + n * 256, 256), 256)
            v = hid[:, wide_cols] + sp[a, :, wide_cols].astype(F32) + own[me, :, cols].astype(F32)
            for i in range(2):
                v = v + sr[i, :, wide_cols].astype(F32) + finals[i, :, cols].astype(F32)
            out[:, wide_cols] = v[0:124].astype(BF)
            return 0

        lax.fori_loop(0, 4, total, 0)
    for copy in sent:
        if id(copy) not in finished:
            copy.wait_send()


def body(
    attn_prefill, decode_held, decode_source, residual, live_rows, expert_ids, replica_pick, w_out, norm_gain, router,
    exp_gate, exp_up, exp_down, shared_gate, shared_up, shared_down,
):
    vmem = pl.BlockSpec(memory_space=pltpu.VMEM)
    smem = pl.BlockSpec(memory_space=pltpu.SMEM)
    hbm = pl.BlockSpec(memory_space=pl.ANY)
    V = pltpu.VMEM
    return pl.pallas_call(
        kernel,
        out_shape=(jax.ShapeDtypeStruct((124, 2048), BF), jax.ShapeDtypeStruct((1,), jnp.int32)),
        in_specs=[vmem, vmem, smem, vmem, vmem, vmem, vmem, hbm, vmem, vmem, hbm, hbm, hbm, hbm, hbm, hbm],
        out_specs=(vmem, smem),
        scratch_shapes=[
            V((2048, 512), BF), V((2048, 1408), BF), V((2048, 1408), BF), V((1408, 2048), BF),
            V((352, 2048), BF), V((352, 2048), BF), V((352, 2048), BF),
            V((128, 2048), F32), V((3, 128, 2048), BF), V((2, 128, 512), BF), V((4, 128, 512), BF),
            V((16, 512), F32), V((16, 512), BF), V((4, 16, 512), BF),
            V((2, 4, 4, 128, 128), BF), V((2, 4, 4, 128, 128), BF),
            V((8, 128), jnp.int32), V((32, 128), F32), V((32, 128), F32), V((4, 8, 128), F32), V((4, 8, 128), F32),
            V((8, 128), F32), V((4, 8, 128), F32), V((4, 8, 128), F32), V((4, 8, 128), F32), V((2, 8, 128), F32),
            V((3, 8, 128), F32),
            V((32, 128), F32), V((32, 128), F32), V((4, 8, 128), F32), V((4, 8, 128), F32),
            V((4, 128, 1024), BF), V((4, 128, 1024), BF),
            V((4, 128, 2048), BF), V((4, 128, 2048), BF), V((2, 64, 2048), BF), V((2, 128, 2048), BF),
            V((384, 512), BF),
            V((2, 4, 96, 1024), BF), V((2, 4, 96, 1024), BF), V((2, 4, 96, 1024), BF), V((2, 4, 96, 1024), BF),
            V((384, 1408), BF), V((384, 1408), BF),
            V((2, 4, 96, 1024), BF), V((2, 4, 96, 1024), BF),
            V((768, 512), F32), V((512, 768), BF), V((512, 768), BF),
            V((4, 128, 1024), BF), V((4, 128, 1024), BF), V((2, 64, 1024), BF), V((2, 64, 1024), BF),
            V((2, 128, 1024), BF), V((2, 128, 1024), BF),
            pltpu.SemaphoreType.DMA((COPIES,)), pltpu.SemaphoreType.DMA((COPIES,)),
            pltpu.SemaphoreType.DMA((7,)), pltpu.SemaphoreType.DMA((4,)),
        ],
        compiler_params=pltpu.CompilerParams(collective_id=0, has_side_effects=True, vmem_limit_bytes=62 << 20),
        cost_estimate=pl.CostEstimate(flops=17_000_000_000, bytes_accessed=26_000_000, transcendentals=2_000_000),
        name="moe",
    )(
        attn_prefill, decode_held, decode_source, residual, live_rows.reshape(1, 1), expert_ids.T, replica_pick, w_out,
        norm_gain.reshape(1, 2048), router.T, exp_gate, exp_up, exp_down, shared_gate, shared_up, shared_down,
    )


def solution(mesh):
    rows = P(("dp", "expert"), None)
    flat = P(("dp", "expert"))
    placed = (
        rows, rows, flat, rows, flat, rows, rows, P(None, "dp"), P(), P(),
        P("expert", None, None), P("expert", None, None), P("expert", None, None),
        P("dp", None), P("dp", None), P("dp", None),
    )
    return jax.shard_map(body, mesh=mesh, in_specs=placed, out_specs=(rows, flat), check_vma=False)
```

```python
import functools

import jax
import jax.numpy as jnp
from jax import lax
from jax.experimental import pallas as pl
from jax.experimental.pallas import tpu as pltpu
from jax.sharding import PartitionSpec as P

EPSILON = 1e-06
MESH = pl.DeviceIdType.MESH
BF = jnp.bfloat16
F32 = jnp.float32
NT = (((1,), (1,)), ((), ()))

GROUPS = dict(
    Z_TOP=2, Z_BOTTOM=2, Z_RET=4, HELD=3, W_PIECE=2, WA_X=3, WA_Y=3, WB_Y=3, WB_X=3, W_CORE=8, CODE_A=3, CODE_B=3, CR_Z=3,
    CR_X=3, CR_Y=3, CR_K=1, PROB_A=3, PROB_B=3, X_AG=6, Y_AG=6, S_AG=6, DIS_A=8, DIS_B=8, S_SUM=6, RET_A=8, RET_B=8, SUM_A=6, SUM_B=6,
)
COPIES = sum(GROUPS.values())
ID = {name: sum(list(GROUPS.values())[:i]) for i, name in enumerate(GROUPS)}


def dot(a, b):
    return jnp.dot(a, b, preferred_element_type=F32)


def iota(shape, dim):
    return lax.broadcasted_iota(jnp.int32, shape, dim)


def kernel(
    pre, held, source, resid, live, ids, pick, w_out_h, gain, router_t, wg_h, wu_h, wd_h, sg_h, su_h, sd_h,
    out, copy_rows,
    w_out, wg, wu, wd, sg, su, sd,
    hid, zb, pb, pr, held_f, held_s, held_all, wo_a, wo_b, idsp, code_a, code_b, ca, cb, svt, crz, crx, cry, crk, crs,
    prob_a, prob_b, pa, pb_b, buf_a, buf_b, sb, sp, s_mid, sr, onehot, s2a, s2b, r2a, r2b, inner_a, inner_b,
    r3a, r3b, wide, wca, wcb, s4a, s4b, mid_a, mid_b, r4a, r4b,
    ss, rs, ws, ls,
):
    a = lax.axis_index("dp")
    c = lax.axis_index("expert")
    x, y, k = c // 8, lax.rem(c // 2, 4), lax.rem(c, 2)

    def at(z_, x_, y_, k_):
        return (z_, (x_ * 4 + y_) * 2 + k_)

    def m4(v):
        return lax.rem(v, 4)

    loads = [
        pltpu.make_async_copy(src, dst, ws.at[i])
        for i, (src, dst) in enumerate(
            [(w_out_h, w_out), (sg_h, sg), (su_h, su), (sd_h, sd), (wg_h.at[0], wg), (wu_h.at[0], wu), (wd_h.at[0], wd)]
        )
    ]
    loads[0].start()

    barrier = pltpu.get_barrier_semaphore()
    peers = [at(m4(a + i), x, y, k) for i in (1, 2, 3)]
    peers += [at(a, x, m4(y + i), lax.rem(k + j, 2)) for i in range(4) for j in range(2) if i or j]
    peers += [at(a, m4(x + i), y, lax.rem(k + j, 2)) for i in (1, 2, 3) for j in range(2)]
    for peer in peers:
        pl.semaphore_signal(barrier, inc=1, device_id=peer, device_id_type=MESH)

    sent, finished = [], set()

    def send(i, src, dst, device):
        copy = pltpu.make_async_remote_copy(
            src_ref=src, dst_ref=dst, send_sem=ss.at[i], recv_sem=rs.at[i], device_id=device, device_id_type=MESH
        )
        copy.start()
        sent.append(copy)
        return copy

    zdev = lambda i: at(i, x, y, k)
    xdev = lambda i: at(a, i, y, k)
    ydev = lambda i: at(a, x, i, k)

    def others(me, base, dev, src, dst):
        return [send(base + i - 1, src(m4(me + i)), dst(m4(me + i)), dev(m4(me + i))) for i in (1, 2, 3)]

    def ring(base, buf, me, dev, half=64):
        right, left = m4(me + 1), m4(me + 3)
        top, bottom = pl.ds(0, half), pl.ds(half, half)
        go = lambda i, slot, part, to: send(base + i, buf.at[slot, part], buf.at[slot, part], dev(to))
        copies = [go(0, me, top, right), go(1, me, bottom, left), go(2, me, bottom, right), go(3, me, top, left)]

        def forward():
            copies[0].wait_recv()
            copies.append(go(4, left, top, right))
            copies[1].wait_recv()
            copies.append(go(5, right, bottom, left))

        return copies, forward

    def ring_sum(base, sums, middle, finals, me, dev):
        right, left, far = m4(me + 1), m4(me + 3), m4(me + 2)
        top, bottom = pl.ds(0, 64), pl.ds(64, 64)
        copies = {}

        def go(i, slot, part, landing, to):
            copies[i] = send(base + i, sums.at[slot, part], landing, dev(to))

        def far_ready():
            go(0, far, top, middle.at[0], right)
            go(1, far, bottom, middle.at[1], left)

        def right_ready():
            go(2, right, bottom, finals.at[0, bottom], right)

        def left_ready():
            go(3, left, top, finals.at[1, top], left)

        def pass_on():
            copies[0].wait_recv()
            sums[right, top, :] = (sums[right, top, :].astype(F32) + middle[0].astype(F32)).astype(BF)
            go(4, right, top, finals.at[0, top], right)
            copies[1].wait_recv()
            sums[left, bottom, :] = (sums[left, bottom, :].astype(F32) + middle[1].astype(F32)).astype(BF)
            go(5, left, bottom, finals.at[1, bottom], left)

        def landed():
            for i in (2, 3, 4, 5):
                copies[i].wait_recv()

        return far_ready, right_ready, left_ready, pass_on, landed

    left, right, opposite = m4(a + 3), m4(a + 1), m4(a + 2)
    top, bottom = pl.ds(0, 64), pl.ds(64, 64)
    zb[0, 0:64, :] = pre[0:64, :]
    for i in range(4):
        held_f[4 * i : 4 * i + 4, :] = held[:, 512 * i : 512 * i + 512].astype(F32)
    held_s[...] = held_f[...].astype(BF)
    held_all[a] = held_s[...]
    loads[0].wait()

    pl.semaphore_wait(barrier, len(peers))

    piece_rows = pl.ds(pl.multiple_of((x * 4 + y) * 128, 128), 128)
    piece_cols = lambda i: pl.ds(pl.multiple_of(k * 256 + i * 128, 128), 128)
    pieces = [send(ID["W_PIECE"], w_out.at[piece_rows, piece_cols(0)], wo_a.at[k, y, x], zdev(opposite))]
    pieces += [send(ID["W_PIECE"] + 1, w_out.at[piece_rows, piece_cols(1)], wo_b.at[k, x, y], zdev(opposite))]
    held_copies = others(a, ID["HELD"], zdev, lambda i: held_s, lambda i: held_all.at[a])

    def both(base, part):
        return [
            send(base, zb.at[0, part], zb.at[1, part], zdev(right)),
            send(base + 1, zb.at[0, part], zb.at[2, part], zdev(left)),
        ]

    tops = both(ID["Z_TOP"], top)
    for load in loads[1:]:
        load.start()

    hid[0:120, :] = pre[...].astype(F32)
    hid[120:128, :] = jnp.zeros((8, 2048), F32)
    row64, col64 = iota((64, 64), 0), iota((64, 64), 1)
    chosen = jnp.full((64, 64), -64, jnp.int32)
    for i in range(4):
        chosen = jnp.where(row64 == 56 + i, source[i] // 4 * 16 + lax.rem(source[i], 4), chosen)
    for copy in pieces:
        copy.wait_recv()
    ax_copies = others(x, ID["WA_X"], xdev, lambda i: wo_a.at[k, y, x], lambda i: wo_a.at[k, y, x])
    by_copies = others(y, ID["WB_Y"], ydev, lambda i: wo_b.at[k, x, y], lambda i: wo_b.at[k, x, y])
    for copy in held_copies:
        copy.wait_recv()
    for i in range(4):
        cols = slice(512 * i, 512 * i + 512)
        picked = dot(jnp.where(col64 == chosen + 4 * i, 1.0, 0.0).astype(BF), held_all[...].reshape(64, 512))
        zb[0, 64:128, cols] = (hid[64:128, cols] + picked).astype(BF)
    bottoms = both(ID["Z_BOTTOM"], bottom)
    for copy in ax_copies:
        copy.wait_recv()
    ay_copies = others(y, ID["WA_Y"], ydev, lambda i: wo_a.at[k, y], lambda i: wo_a.at[k, y])
    for copy in by_copies:
        copy.wait_recv()
    bx_copies = others(x, ID["WB_X"], xdev, lambda i: wo_b.at[k, x], lambda i: wo_b.at[k, x])

    def to_sibling(i, wo, slot):
        return send(ID["W_CORE"] + i, wo.at[k, slot], wo.at[k, slot], at(a, x, y, 1 - k))

    core_copies = [to_sibling(0, wo_a, y), to_sibling(4, wo_b, x)]

    idsp[...] = jnp.full((8, 128), -1, jnp.int32)
    idsp[0:6, 0:124] = ids[...]
    lane = iota((32, 128), 1)
    row = iota((32, 128), 0)
    alive = (lane < live[...]) | (lane >= 120)
    before = jnp.where(iota((128, 128), 0) < iota((128, 128), 1), 1.0, 0.0).astype(BF)

    def match(expert):
        hit = idsp[0:1, :] == expert
        for i in range(1, 6):
            hit = hit | (idsp[i : i + 1, :] == expert)
        return jnp.where(hit & alive, 1.0, 0.0)

    hits = match(row)
    ranks = dot(hits.astype(BF), before)
    code_a[...] = jnp.where(hits > 0.5, ranks + (24 * x).astype(F32), -1.0)
    hits_b = match(lax.rem(row // 2, 4) * 8 + row // 8 * 2 + lax.rem(row, 2))
    ranks_b = dot(hits_b.astype(BF), before)
    code_b[...] = jnp.where(hits_b > 0.5, ranks_b + (24 * y).astype(F32), -1.0)

    def tile(ref, i):
        return ref.at[pl.ds(pl.multiple_of(i * 8, 8), 8)]

    ca[x] = code_a[pl.ds(pl.multiple_of(x * 8, 8), 8), :]
    cb[y] = code_b[pl.ds(pl.multiple_of(y * 8, 8), 8), :]
    code_copies = others(x, ID["CODE_A"], xdev, lambda i: tile(code_a, i), lambda i: ca.at[x])
    code_copies += others(y, ID["CODE_B"], ydev, lambda i: tile(code_b, i), lambda i: cb.at[y])

    counts = lax.dot_general(jnp.ones((8, 128), BF), hits.astype(BF), NT, preferred_element_type=F32)
    copy_index = iota((8, 32), 0)
    offset = lax.rem(copy_index - pick[...] + 4, 4)
    served = (counts.astype(jnp.int32) - offset + 3) // 4
    svt[...] = jnp.zeros((8, 128), F32)
    svt[:, 0:32] = jnp.where(copy_index < 4, served, 0).astype(F32)
    crz[a] = svt[...]
    cr_copies = others(a, ID["CR_Z"], zdev, lambda i: svt, lambda i: crz.at[a])

    pr[a] = dot(zb[0], w_out[...]).astype(BF)
    returns = []

    def project(i, copies, part):
        for copy in copies:
            copy.wait_recv()
        rows = jnp.concatenate([zb[1, part, :], zb[2, part, :]], axis=0)
        pb[i] = dot(rows, w_out[...]).astype(BF)
        returns.append(send(ID["Z_RET"] + 2 * i, pb.at[i, top], pr.at[a, part], zdev(left)))
        returns.append(send(ID["Z_RET"] + 2 * i + 1, pb.at[i, bottom], pr.at[a, part], zdev(right)))

    project(0, tops, top)
    hid[120:128, :] = jnp.zeros((8, 2048), F32)
    hid[0:124, :] = resid[...].astype(F32)
    for copy in cr_copies:
        copy.wait_recv()
    crs[0] = crz[0] + crz[1] + crz[2] + crz[3]
    crx[x] = crs[0]
    cr_copies = others(x, ID["CR_X"], xdev, lambda i: crs.at[0], lambda i: crx.at[x])
    for i in (1, 2, 3):
        ay_copies[i - 1].wait_recv()
        core_copies.append(to_sibling(i, wo_a, m4(y + 4 - i)))
        bx_copies[i - 1].wait_recv()
        core_copies.append(to_sibling(4 + i, wo_b, m4(x + 4 - i)))
    project(1, bottoms, bottom)

    def far(core):
        v = jnp.zeros((128, 256), F32)
        for i in range(8):
            m, n = i // 2, i % 2 * 2
            rows = [jnp.concatenate([wo_a[core, j, m], wo_b[core, m, j]], axis=1) for j in (n, n + 1)]
            v = v + dot(zb[0, :, 256 * i : 256 * i + 256], jnp.concatenate(rows, axis=0))
        pr[opposite, :, pl.ds(pl.multiple_of(core * 256, 256), 256)] = v.astype(BF)

    far(k)
    for copy in core_copies:
        copy.wait_recv()
    far(1 - k)

    for copy in returns:
        copy.wait_recv()
    for i in range(4):
        cols = slice(i * 512, i * 512 + 512)
        hid[:, cols] = hid[:, cols] + pr[i].astype(F32)

    def norm(i, _):
        rows = pl.ds(pl.multiple_of(i * 16, 16), 16)
        v = hid[rows, :]
        scale = lax.rsqrt(jnp.mean(v * v, axis=1, keepdims=True) + EPSILON)
        normed = (v * scale * gain[...]).astype(BF)
        buf_a[x, rows, :] = normed[:, 0:1024]
        buf_b[y, rows, :] = normed[:, 1024:2048]
        sb[a, rows, :] = normed
        return 0

    lax.fori_loop(0, 8, norm, 0)
    x_copies, x_forward = ring(ID["X_AG"], buf_a, x, xdev)
    y_copies, y_forward = ring(ID["Y_AG"], buf_b, y, ydev)
    s_copies, s_forward = ring(ID["S_AG"], sb, a, zdev)

    logits = lax.dot_general(router_t[...], sb[a], NT, preferred_element_type=F32)
    powers = jnp.exp(logits - jnp.max(logits, axis=0, keepdims=True))
    prob_a[...] = powers / jnp.sum(powers, axis=0, keepdims=True)
    for i in range(16):
        j = i % 4 * 4 + i // 4
        prob_b[2 * i : 2 * i + 2, :] = prob_a[2 * j : 2 * j + 2, :]
    pa[x] = prob_a[pl.ds(pl.multiple_of(x * 8, 8), 8), :]
    pb_b[y] = prob_b[pl.ds(pl.multiple_of(y * 8, 8), 8), :]
    prob_copies = others(x, ID["PROB_A"], xdev, lambda i: tile(prob_a, i), lambda i: pa.at[x])
    prob_copies += others(y, ID["PROB_B"], ydev, lambda i: tile(prob_b, i), lambda i: pb_b.at[y])

    x_forward()
    y_forward()
    s_forward()
    for copy in cr_copies:
        copy.wait_recv()
    crs[1] = crx[0] + crx[1] + crx[2] + crx[3]
    cry[y] = crs[1]
    cr_copies = others(y, ID["CR_Y"], ydev, lambda i: crs.at[1], lambda i: cry.at[y])
    for copy in code_copies:
        copy.wait_recv()

    for load in loads[1:4]:
        load.wait()

    def shared(i):
        rows = sb[i]
        gate = lax.dot_general(rows, sg[...], NT, preferred_element_type=F32)
        up = lax.dot_general(rows, su[...], NT, preferred_element_type=F32)
        hidden_units = (gate / (1.0 + jnp.exp(-gate)) * up).astype(BF)

        def columns(n, _):
            cols = pl.ds(pl.multiple_of(n * 512, 512), 512)
            sp[i, :, cols] = dot(hidden_units, sd[:, cols]).astype(BF)
            return 0

        lax.fori_loop(0, 4, columns, 0, unroll=True)

    def shared_of(i, parts):
        for part in parts:
            s_copies[part].wait_recv()
        shared(m4(a + i))

    s_far, s_right, s_left, s_pass, s_landed = ring_sum(ID["S_SUM"], sp, s_mid, sr, a, zdev)
    shared(a)

    slot96 = iota((96, 512), 0).astype(F32)

    def codes(ref, i):
        return jnp.concatenate([ref[s, pl.ds(i, 1), :] for s in range(4)], axis=1)

    locals_ = []

    def dispatch(base, step, core, code, buf, slots, landing, me, dev, group):
        for i in range(4):
            onehot[96 * i : 96 * i + 96, :] = jnp.where(slot96 == codes(code, 2 * i + core), 1.0, 0.0).astype(BF)

        def columns(n, _):
            cols = pl.ds(pl.multiple_of(n * 256, 256), 256)
            rows = buf[:, :, cols].reshape(512, 256)
            slots[core, :, :, cols] = dot(onehot[...], rows).astype(BF).reshape(4, 96, 256)
            return 0

        lax.fori_loop(0, 4, columns, 0, unroll=True)

        def start(i):
            to = m4(me + i)
            if step == 0 and i == 0:
                copy = pltpu.make_async_copy(slots.at[core, to], landing.at[k, me], ls.at[base])
                copy.start()
                locals_.append(copy)
            else:
                arrive[step].append(send(group + 4 * step + i, slots.at[core, to], landing.at[k, me], dev(to, core)))

        return start

    col_dev = lambda i, core: at(a, x, i, core)
    row_dev = lambda i, core: at(a, i, y, core)
    for copy in x_copies[2:]:
        copy.wait_recv()
    arrive = [[], []]
    first_a = dispatch(0, 0, k, ca, buf_a, s2a, r2a, y, col_dev, ID["DIS_A"])
    for i in range(4):
        first_a(i)
    for copy in y_copies[2:]:
        copy.wait_recv()
    first_b = dispatch(1, 0, k, cb, buf_b, s2b, r2b, x, row_dev, ID["DIS_B"])
    for i in range(4):
        first_b(i)
    second_a = dispatch(0, 1, 1 - k, ca, buf_a, s2a, r2a, y, col_dev, ID["DIS_A"])
    second_b = dispatch(1, 1, 1 - k, cb, buf_b, s2b, r2b, x, row_dev, ID["DIS_B"])
    second_a(0)
    second_b(0)

    shared_of(3, (2,))
    s_left()
    shared_of(1, (3,))
    s_right()

    for i in (1, 2, 3):
        for copy, second in ((arrive[0][i - 1], second_a), (arrive[0][i + 2], second_b)):
            copy.wait_send()
            finished.add(id(copy))
            second(i)

    for copy in cr_copies:
        copy.wait_recv()
    crs[2] = cry[0] + cry[1] + cry[2] + cry[3]
    crk[k] = crs[2]
    cr_copy = send(ID["CR_K"], crs.at[2], crk.at[k], at(a, x, y, 1 - k))

    for load in loads[4:]:
        load.wait()

    def swapped(v):
        return jnp.concatenate([v[(j * 4 + i) * 24 : (j * 4 + i) * 24 + 24] for i in range(4) for j in range(4)], axis=0)

    def expert(step, core):
        for copy in arrive[step]:
            copy.wait_recv()
        if step == 0:
            for copy in locals_:
                copy.wait()

        def up(cols):
            first = jnp.concatenate([wg[0:1024, cols], wu[0:1024, cols]], axis=1)
            second = jnp.concatenate([wg[1024:2048, cols], wu[1024:2048, cols]], axis=1)
            h = dot(r2a[core].reshape(384, 1024), first) + swapped(dot(r2b[core].reshape(384, 1024), second))
            width = h.shape[1] // 2
            gate = h[:, 0:width]
            inner = gate / (1.0 + jnp.exp(-gate)) * h[:, width : 2 * width]
            inner_a[:, cols] = inner.astype(BF)
            inner_b[:, cols] = swapped(inner).astype(BF)

        for first in range(0, 1408, 256):
            up(slice(first, min(first + 256, 1408)))
        for copy in arrive[step]:
            if id(copy) not in finished:
                copy.wait_send()
                finished.add(id(copy))
        copies = []
        for group, inner, slots, landing, me, dev, first in (
            (ID["RET_A"], inner_a, s2a, r3a, y, col_dev, 0),
            (ID["RET_B"], inner_b, s2b, r3b, x, row_dev, 1024),
        ):

            for n in (0, 512):
                out_cols = dot(inner[...], wd[:, first + n : first + n + 512])
                slots[core, :, :, n : n + 512] = out_cols.astype(BF).reshape(4, 96, 512)
            for i in range(4):
                to = m4(me + i)
                if step == 0 and i == 0:
                    copy = pltpu.make_async_copy(slots.at[core, to], landing.at[k, me], ls.at[2 + (group == ID["RET_B"])])
                    copy.start()
                    locals_.append(copy)
                    continue
                copies.append(send(group + 4 * step + i, slots.at[core, to], landing.at[k, me], dev(to, core)))
        return copies

    back = expert(0, k)
    back += expert(1, 1 - k)
    shared_of(2, (4, 5))
    s_far()
    back_a, back_b = [back[i] for i in (0, 1, 2, 6, 7, 8, 9)], [back[i] for i in (3, 4, 5, 10, 11, 12, 13)]

    for copy in prob_copies:
        copy.wait_recv()

    def weights(code, prob, into):
        for i in range(8):
            e = lax.rem(i, 4) * 2 + i // 4
            hit = slot96 == codes(code, e)
            wide[96 * i : 96 * i + 96, :] = jnp.where(hit, codes(prob, e), 0.0)
        into[...] = wide[...].T.astype(BF)

    weights(ca, pa, wca)
    weights(cb, pb_b, wcb)

    s_pass()

    def combine(wc, landed, sums, i):
        rows = pl.ds(pl.multiple_of(i * 128, 128), 128)
        sums[i] = dot(wc[rows, :], landed[...].reshape(768, 1024)).astype(BF)

    a_far, a_right, a_left, a_pass, a_landed = ring_sum(ID["SUM_A"], s4a, mid_a, r4a, x, xdev)
    b_far, b_right, b_left, b_pass, b_landed = ring_sum(ID["SUM_B"], s4b, mid_b, r4b, y, ydev)
    for copies, local, part, me, ready in ((back_a, locals_[2], (wca, r3a, s4a), x, a_far), (back_b, locals_[3], (wcb, r3b, s4b), y, b_far)):
        for copy in copies:
            copy.wait_recv()
        local.wait()
        combine(*part, m4(me + 2))
        ready()
    for part, me, rest in (((wca, r3a, s4a), x, (a_right, a_left)), ((wcb, r3b, s4b), y, (b_right, b_left))):
        combine(*part, m4(me + 1))
        rest[0]()
        combine(*part, m4(me + 3))
        rest[1]()
    a_pass()
    b_pass()
    combine(wca, r3a, s4a, x)
    combine(wcb, r3b, s4b, y)

    cr_copy.wait_recv()
    served_all = crk[0] + crk[1]
    mine = (iota((8, 128), 0) == a) & (iota((8, 128), 1) == c)
    copy_rows[0] = jnp.sum(jnp.where(mine, served_all, 0.0)).astype(jnp.int32)

    s_landed()
    for landed, own, finals, me, first in ((a_landed, s4a, r4a, x, 0), (b_landed, s4b, r4b, y, 1024)):
        landed()

        def total(n, _):
            cols = pl.ds(pl.multiple_of(n * 256, 256), 256)
            wide_cols = pl.ds(pl.multiple_of(first + n * 256, 256), 256)
            v = hid[:, wide_cols] + sp[a, :, wide_cols].astype(F32) + own[me, :, cols].astype(F32)
            for i in range(2):
                v = v + sr[i, :, wide_cols].astype(F32) + finals[i, :, cols].astype(F32)
            out[:, wide_cols] = v[0:124].astype(BF)
            return 0

        lax.fori_loop(0, 4, total, 0)
    for copy in sent:
        if id(copy) not in finished:
            copy.wait_send()


def body(
    attn_prefill, decode_held, decode_source, residual, live_rows, expert_ids, replica_pick, w_out, norm_gain, router,
    exp_gate, exp_up, exp_down, shared_gate, shared_up, shared_down,
):
    vmem = pl.BlockSpec(memory_space=pltpu.VMEM)
    smem = pl.BlockSpec(memory_space=pltpu.SMEM)
    hbm = pl.BlockSpec(memory_space=pl.ANY)
    V = pltpu.VMEM
    return pl.pallas_call(
        kernel,
        out_shape=(jax.ShapeDtypeStruct((124, 2048), BF), jax.ShapeDtypeStruct((1,), jnp.int32)),
        in_specs=[vmem, vmem, smem, vmem, vmem, vmem, vmem, hbm, vmem, vmem, hbm, hbm, hbm, hbm, hbm, hbm],
        out_specs=(vmem, smem),
        scratch_shapes=[
            V((2048, 512), BF), V((2048, 1408), BF), V((2048, 1408), BF), V((1408, 2048), BF),
            V((352, 2048), BF), V((352, 2048), BF), V((352, 2048), BF),
            V((128, 2048), F32), V((3, 128, 2048), BF), V((2, 128, 512), BF), V((4, 128, 512), BF),
            V((16, 512), F32), V((16, 512), BF), V((4, 16, 512), BF),
            V((2, 4, 4, 128, 128), BF), V((2, 4, 4, 128, 128), BF),
            V((8, 128), jnp.int32), V((32, 128), F32), V((32, 128), F32), V((4, 8, 128), F32), V((4, 8, 128), F32),
            V((8, 128), F32), V((4, 8, 128), F32), V((4, 8, 128), F32), V((4, 8, 128), F32), V((2, 8, 128), F32),
            V((3, 8, 128), F32),
            V((32, 128), F32), V((32, 128), F32), V((4, 8, 128), F32), V((4, 8, 128), F32),
            V((4, 128, 1024), BF), V((4, 128, 1024), BF),
            V((4, 128, 2048), BF), V((4, 128, 2048), BF), V((2, 64, 2048), BF), V((2, 128, 2048), BF),
            V((384, 512), BF),
            V((2, 4, 96, 1024), BF), V((2, 4, 96, 1024), BF), V((2, 4, 96, 1024), BF), V((2, 4, 96, 1024), BF),
            V((384, 1408), BF), V((384, 1408), BF),
            V((2, 4, 96, 1024), BF), V((2, 4, 96, 1024), BF),
            V((768, 512), F32), V((512, 768), BF), V((512, 768), BF),
            V((4, 128, 1024), BF), V((4, 128, 1024), BF), V((2, 64, 1024), BF), V((2, 64, 1024), BF),
            V((2, 128, 1024), BF), V((2, 128, 1024), BF),
            pltpu.SemaphoreType.DMA((COPIES,)), pltpu.SemaphoreType.DMA((COPIES,)),
            pltpu.SemaphoreType.DMA((7,)), pltpu.SemaphoreType.DMA((4,)),
        ],
        compiler_params=pltpu.CompilerParams(collective_id=0, has_side_effects=True, vmem_limit_bytes=62 << 20),
        cost_estimate=pl.CostEstimate(flops=17_000_000_000, bytes_accessed=26_000_000, transcendentals=2_000_000),
        name="moe",
    )(
        attn_prefill, decode_held, decode_source, residual, live_rows.reshape(1, 1), expert_ids.T, replica_pick, w_out,
        norm_gain.reshape(1, 2048), router.T, exp_gate, exp_up, exp_down, shared_gate, shared_up, shared_down,
    )


def solution(mesh):
    rows = P(("dp", "expert"), None)
    flat = P(("dp", "expert"))
    placed = (
        rows, rows, flat, rows, flat, rows, rows, P(None, "dp"), P(), P(),
        P("expert", None, None), P("expert", None, None), P("expert", None, None),
        P("dp", None), P("dp", None), P("dp", None),
    )
    return jax.shard_map(body, mesh=mesh, in_specs=placed, out_specs=(rows, flat), check_vma=False)
```
